128 devices in a mesh: gx: 8 (over x_hi, y), gy: 16 (over z, x_lo, core).
Axes of the slice: x: 4 (x_hi: 2, x_lo: 2; x = x_hi * 2 + x_lo), y: 4, z: 4, core: 2. Of those that a mesh axis runs over, the one named last changes fastest.
Arguments:
- start_potentials: float32 [128, 256, 16, 128], P('gx', 'gy'), may hold values from -6 to 6
- conductivity: float32 [128, 256, 16], P('gx', 'gy'), may hold values from 0.2 to 5
- electrodes: int32 [128, 2], replicated, may hold values from 0 to 32767
- coarse_inverse: float32 [4096, 4096], P(('gx', 'gy')), as said below
Outputs:
- potentials: float32 [128, 256, 16, 128], P('gx', 'gy')
- residual: float32 [128, 256, 16, 128], P('gx', 'gy')
The draws below stay inside these ranges and needn't reach their ends.
Inputs may be any that keep to these rules, and one draw needn't show every extreme that they name: electrodes[f, k] is the index x * 256 + y of a cell at depth 0. coarse_inverse is exactly symmetric.
All inputs are finite; a program needn't handle non-finite values.
Results may differ from the reference program's by a relative error of at most 0.0003.
Values sent between devices are 32-bit elements; how exact they have to be, the bound alone decides.
A program may use at most 128 MiB of HBM per device.

```python
import math
import jax
import jax.numpy as jnp
from jax import lax

BX = 16
BY = 16
NZ = 16
FIELDS = 128
DELTA = 2
SWEEPS = 4
ITERS = 2
CSX = 4
CSY = 4
CSZ = 2
NX = 128
NY = 256
COARSE = 4096
N_GX = 8
N_GY = 16


def draw_coarse_inverse(key, part):
    key = jax.random.fold_in(key, 7)
    base = jax.random.normal(key, (COARSE, COARSE), jnp.float32)
    symmetric = (base + base.T) * (0.006 / math.sqrt(2.0 * COARSE))
    return symmetric + 0.02 * jnp.eye(COARSE, dtype=jnp.float32)


def set_ends(values, stream_key, low, top_value):
    extent = values.shape
    place = [jax.random.randint(jax.random.fold_in(stream_key, axis), (), 0, extent[axis]) for axis in range(len(extent))]
    values = values.at[tuple(place)].set(low)
    longest = extent.index(max(extent))
    place[longest] = (place[longest] + 1) % extent[longest]
    return values.at[tuple(place)].set(top_value)


def shard_levels(rng, dims, split, low, high):
    loudness, own = 1.0, jax.random.fold_in(rng, 6)
    for position, parts in split:
        draws = jnp.exp(jax.random.uniform(jax.random.fold_in(own, position), (parts,), jnp.float32, low / len(split), high / len(split)))
        loudness = loudness * jnp.repeat(draws, dims[position] // parts).reshape([-1 if axis == position else 1 for axis in range(len(dims))])
    return loudness


def normal_values(key, shape, scale, limit, pieces=(), kind=jnp.bfloat16):
    array = jax.random.normal(key, shape, jnp.float32) * scale
    if len(pieces) > 0:
        array = shard_levels(key, shape, pieces, -0.22, 0.18) * array
    return jnp.clip(array, min=-limit, max=limit).astype(kind)


def setup_inputs(seed: int = 0) -> dict:
    arg_keys = jax.random.split(jax.random.key(seed), 5)
    return {
        "start_potentials": normal_values(arg_keys[0], (NX, NY, NZ, FIELDS), 1.0, 6.0, ((0, 8), (1, 16)), jnp.float32),
        "conductivity": jnp.clip(jnp.exp(math.log(5.0) - 3.218876 * jax.random.uniform(arg_keys[1], (NX, NY, NZ), jnp.float32) ** shard_levels(arg_keys[1], (NX, NY, NZ), ((0, 8), (1, 16)), -0.2, 0.2)), 0.2, 5.0),
        "electrodes": set_ends(jax.random.randint(arg_keys[2], (FIELDS, 2), 0, NX * NY), jax.random.fold_in(arg_keys[2], 1), 0, (NX * NY) - 1).astype(jnp.int32),
        "coarse_inverse": draw_coarse_inverse(jax.random.fold_in(arg_keys[4], 71), 0),
    }


OMEGA = 0.7
CURRENT = 8.0


def face_terms(sigma_pad, inside):
    centre = sigma_pad[1:-1, 1:-1]
    layers = centre.shape[2]
    zero_layer = jnp.zeros(centre.shape[:2] + (1,), centre.dtype)
    deeper = jnp.concatenate([centre[:, :, 1:], zero_layer], axis=2)
    shallower = jnp.concatenate([zero_layer, centre[:, :, :-1]], axis=2)
    surface = (jnp.arange(layers) > 0).astype(centre.dtype)
    west_face = 0.5 * (centre + sigma_pad[:-2, 1:-1]) * inside
    east_face = 0.5 * (centre + sigma_pad[2:, 1:-1]) * inside
    south_face = 0.5 * (centre + sigma_pad[1:-1, :-2]) * inside
    north_face = 0.5 * (centre + sigma_pad[1:-1, 2:]) * inside
    lower_face = 0.5 * (centre + deeper) * inside
    upper_face = 0.5 * (centre + shallower) * inside * surface
    return (west_face, east_face, south_face, north_face, lower_face, upper_face)


def apply_op(couplings, padded):
    west_face, east_face, south_face, north_face, lower_face, upper_face = [c[..., None] for c in couplings]
    values = padded[1:-1, 1:-1]
    zero_layer = jnp.zeros(values.shape[:2] + (1, values.shape[3]), values.dtype)
    deeper = jnp.concatenate([values[:, :, 1:], zero_layer], axis=2)
    shallower = jnp.concatenate([zero_layer, values[:, :, :-1]], axis=2)
    total_face = west_face + east_face + south_face + north_face + lower_face + upper_face
    beside = (west_face * padded[:-2, 1:-1] + east_face * padded[2:, 1:-1] + south_face * padded[1:-1, :-2]
              + north_face * padded[1:-1, 2:] + lower_face * deeper + upper_face * shallower)
    return total_face * values - beside


def local_solve(couplings, inside, residual_part):
    diagonal = couplings[0] + couplings[1] + couplings[2] + couplings[3] + couplings[4] + couplings[5] + (1.0 - inside)
    step_size = (OMEGA / diagonal)[..., None]
    estimate = step_size * residual_part
    for sweep_index in range(SWEEPS - 1):
        widened = jnp.pad(estimate, ((1, 1), (1, 1), (0, 0), (0, 0)))
        estimate = estimate + step_size * (residual_part - apply_op(couplings, widened))
    return estimate


def forcing_field(row_global, col_global, inside_plane, electrodes, grid_cols, layers):
    cell_index = row_global[:, None] * grid_cols + col_global[None, :]
    source_hit = (cell_index[:, :, None] == electrodes[None, None, :, 0]).astype(inside_plane.dtype)
    sink_hit = (cell_index[:, :, None] == electrodes[None, None, :, 1]).astype(inside_plane.dtype)
    surface_term = CURRENT * (source_hit - sink_hit) * inside_plane[:, :, None]
    below = jnp.zeros(surface_term.shape[:2] + (layers - 1, surface_term.shape[2]), surface_term.dtype)
    return jnp.concatenate([surface_term[:, :, None, :], below], axis=2)


def pad_plane(values, width):
    extra = [(0, 0)] * (values.ndim - 2)
    return jnp.pad(values, [(width, width), (width, width)] + extra)


def reference(start_potentials, conductivity, electrodes, coarse_inverse):
    fdtype = start_potentials.dtype
    ones_grid = jnp.ones((NX, NY, NZ), fdtype)
    couplings_all = face_terms(pad_plane(conductivity, 1), ones_grid)
    row_global = jnp.arange(NX, dtype=jnp.int32)
    col_global = jnp.arange(NY, dtype=jnp.int32)
    forcing = forcing_field(row_global, col_global, jnp.ones((NX, NY), fdtype), electrodes, NY, NZ)
    potentials = start_potentials
    residual = forcing - apply_op(couplings_all, pad_plane(potentials, 1))
    sigma_big = pad_plane(conductivity, DELTA + 1)
    mask_big = pad_plane(ones_grid, DELTA)
    ext_rows = BX + 2 * DELTA
    ext_cols = BY + 2 * DELTA
    zero_index = jnp.zeros((), jnp.int32)
    for iteration in range(ITERS):
        residual_big = pad_plane(residual, DELTA)

        def tile_solve(index):
            row_block = (index // N_GY).astype(jnp.int32)
            col_block = (index % N_GY).astype(jnp.int32)
            row_start = row_block * BX
            col_start = col_block * BY
            sigma_tile = lax.dynamic_slice(sigma_big, (row_start, col_start, zero_index), (ext_rows + 2, ext_cols + 2, NZ))
            mask_tile = lax.dynamic_slice(mask_big, (row_start, col_start, zero_index), (ext_rows, ext_cols, NZ))
            residual_tile = lax.dynamic_slice(residual_big, (row_start, col_start, zero_index, zero_index), (ext_rows, ext_cols, NZ, FIELDS))
            couplings = face_terms(sigma_tile, mask_tile)
            estimate = local_solve(couplings, mask_tile, residual_tile)
            return estimate[DELTA:DELTA + BX, DELTA:DELTA + BY]

        tiles = lax.map(tile_solve, jnp.arange(N_GX * N_GY, dtype=jnp.int32))
        fine = tiles.reshape(N_GX, N_GY, BX, BY, NZ, FIELDS).transpose(0, 2, 1, 3, 4, 5).reshape(NX, NY, NZ, FIELDS)
        grouped = residual.reshape(N_GX, CSX, BX // CSX, N_GY, CSY, BY // CSY, CSZ, NZ // CSZ, FIELDS)
        coarse_res = jnp.sum(grouped, axis=(2, 5, 7)).transpose(0, 2, 1, 3, 4, 5).reshape(COARSE, FIELDS)
        coarse_corr = jnp.dot(coarse_inverse, coarse_res, precision=lax.Precision.HIGHEST, preferred_element_type=fdtype)
        blocks = coarse_corr.reshape(N_GX, N_GY, CSX, CSY, CSZ, FIELDS).transpose(0, 2, 1, 3, 4, 5)
        spread = jnp.broadcast_to(blocks[:, :, None, :, :, None, :, None, :],
                                  (N_GX, CSX, BX // CSX, N_GY, CSY, BY // CSY, CSZ, NZ // CSZ, FIELDS))
        correction = fine + spread.reshape(NX, NY, NZ, FIELDS)
        potentials = potentials + correction
        residual = residual - apply_op(couplings_all, pad_plane(correction, 1))
    return potentials, residual
```

```python
import jax
import jax.numpy as jnp
from jax import lax
from jax.experimental import pallas as pl
from jax.experimental.pallas import tpu as pltpu
from jax.sharding import PartitionSpec as P

OMEGA = 0.7
CURRENT = 8.0
ITERS = 2
NI, NJ = 8, 16
B = 16
F = 128
E2 = B + 4
BLK = 32
MESH = pl.DeviceIdType.MESH
F32 = jnp.float32

SIDES = ((-1, 0), (1, 0), (0, -1), (0, 1))
CORNERS = ((-1, -1), (-1, 1), (1, -1), (1, 1))
AROUND = SIDES + CORNERS


def stencil(e, kx, ky, kz, x, y, p, memo):
    total = kx(x, y, p) * e(x - 1, y, p) + kx(x + 1, y, p) * e(x + 1, y, p)
    total = total + (ky(x, y, p) * e(x, y - 1, p) + ky(x, y + 1, p) * e(x, y + 1, p))
    other = e(x, y, 1 - p)
    if p == 0:
        across = pltpu.roll(kz(x, y, 1) * other, 1, 0)
    else:
        across = kz(x, y, 1) * pltpu.roll(other, 7, 0)
    return total + (kz(x, y, 0) * other + across)


def reader(ref, x0, y0, dx, dy):
    held = {}

    def get(x, y, p):
        key = (x, y, p)
        if key not in held:
            held[key] = ref[x0 + (x + dx), y0 + (y + dy), p]
        return held[key]

    return get


def blocks(x_lo, x_n, y_lo, y_n, xb, yb, body):
    def outer(n, carry):
        ix = n // (y_n // yb)
        iy = n % (y_n // yb)
        body(x_lo + ix * xb, y_lo + iy * yb)
        return carry

    lax.fori_loop(0, (x_n // xb) * (y_n // yb), outer, 0)


def kernel(
    v_hbm, cond_ref, elec_ref, cinv_hbm,
    pot_hbm, res_hbm,
    sig, sig_t, sig_b, v_nat, v_per, rr, bb, e_a, e_b, cc, kx, ky, kz, st, dg, res_nat,
    cblk, crow, gath, part, recv, pro, acc,
    sig_s, sig_r, v_s, v_r, c_s, c_r, ag_s, ag_r, rs_s, rs_r, r_s, r_r, h_s, h_r, loc,
):
    i = lax.axis_index("gx")
    j = lax.axis_index("gy")

    def there(dx, dy):
        ok = None
        for d, pos, n in ((dx, i, NI), (dy, j, NJ)):
            if d:
                term = (pos > 0) if d < 0 else (pos < n - 1)
                ok = term if ok is None else ok & term
        return ok

    own_v = pltpu.make_async_copy(v_hbm, v_nat.at[pl.ds(1, B), pl.ds(1, B)], loc.at[0])
    own_v.start()
    own_c = pltpu.make_async_copy(
        cinv_hbm.at[:, pl.ds(i * 512, 512)], cblk.at[pl.ds(i * BLK, BLK)], loc.at[1]
    )
    own_c.start()
    own_s = pltpu.make_async_copy(cond_ref, sig.at[pl.ds(3, B), pl.ds(8, B)], loc.at[2])
    own_s.start()

    bar = pltpu.get_barrier_semaphore()

    def greet_j(k, carry):
        pl.semaphore_signal(bar, inc=1, device_id=(i, lax.rem(j + k, NJ)), device_id_type=MESH)
        return carry

    lax.fori_loop(1, NJ, greet_j, 0)

    def greet_i(k, carry):
        pl.semaphore_signal(bar, inc=1, device_id=(lax.rem(i + k, NI), j), device_id_type=MESH)
        return carry

    lax.fori_loop(1, NI, greet_i, 0)
    count = jnp.int32(NJ - 1 + NI - 1)
    for dx, dy in CORNERS:
        ok = there(dx, dy)

        @pl.when(ok)
        def _():
            pl.semaphore_signal(bar, inc=1, device_id=(i + dx, j + dy), device_id_type=MESH)

        count = count + jnp.where(ok, 1, 0)
    pl.semaphore_wait(bar, count)

    def halo(dirs, make, what):
        for n, (dx, dy) in enumerate(dirs):
            if what in ("start", "sent"):

                @pl.when(there(dx, dy))
                def _():
                    copy = make(n, dx, dy)
                    copy.start() if what == "start" else copy.wait_send()

            else:

                @pl.when(there(-dx, -dy))
                def _():
                    make(n, dx, dy).wait_recv()

    def sig_copy(n, dx, dy):
        xs = {-1: (3, 3, 19), 0: (3, 16, 3), 1: (16, 3, 0)}[dx]
        ys = {-1: (8, 8, 24), 0: (8, 16, 8), 1: (16, 8, 0)}[dy]
        src = cond_ref.at[pl.ds(xs[0] - 3, xs[1]), pl.ds(ys[0] - 8, ys[1])]
        dst = sig.at[pl.ds(xs[2], xs[1]), pl.ds(ys[2], ys[1])]
        return pltpu.make_async_remote_copy(
            src_ref=src, dst_ref=dst, send_sem=sig_s.at[n], recv_sem=sig_r.at[n],
            device_id=(i + dx, j + dy), device_id_type=MESH)

    def edge(d, width, margin):
        return {
            -1: (margin, width, margin + B),
            0: (margin, B, margin),
            1: (margin + B - width, width, margin - width),
        }[d]

    def v_copy(n, dx, dy):
        xs, ys = edge(dx, 1, 1), edge(dy, 1, 1)
        return pltpu.make_async_remote_copy(
            src_ref=v_hbm.at[pl.ds(xs[0] - 1, xs[1]), pl.ds(ys[0] - 1, ys[1])],
            dst_ref=v_nat.at[pl.ds(xs[2], xs[1]), pl.ds(ys[2], ys[1])],
            send_sem=v_s.at[n], recv_sem=v_r.at[n],
            device_id=(i + dx, j + dy), device_id_type=MESH)

    def r_copy(it):
        def make(n, dx, dy):
            xs, ys = edge(dx, 2, 2), edge(dy, 2, 2)
            return pltpu.make_async_remote_copy(
                src_ref=rr.at[it, pl.ds(xs[0], xs[1]), pl.ds(ys[0], ys[1])],
                dst_ref=rr.at[it, pl.ds(xs[2], xs[1]), pl.ds(ys[2], ys[1])],
                send_sem=r_s.at[it, n], recv_sem=r_r.at[it, n],
                device_id=(i + dx, j + dy), device_id_type=MESH)
        return make

    def h_copy(it):
        def make(n, dx, dy):
            xs, ys = edge(dx, 1, 1), edge(dy, 1, 1)
            return pltpu.make_async_remote_copy(
                src_ref=cc.at[it, pl.ds(xs[0], xs[1]), pl.ds(ys[0], ys[1])],
                dst_ref=cc.at[it, pl.ds(xs[2], xs[1]), pl.ds(ys[2], ys[1])],
                send_sem=h_s.at[it, n], recv_sem=h_r.at[it, n],
                device_id=(i + dx, j + dy), device_id_type=MESH)
        return make

    halo(AROUND, sig_copy, "start")
    halo(SIDES, v_copy, "start")

    def c_copy(k, source):
        to = lax.rem(i + k, NI)
        return pltpu.make_async_remote_copy(
            src_ref=cinv_hbm.at[:, pl.ds(to * 512, 512)],
            dst_ref=cblk.at[pl.ds(source * BLK, BLK)],
            send_sem=c_s.at[k], recv_sem=c_r.at[k],
            device_id=(to, j), device_id_type=MESH)

    def c_start(k, carry):
        c_copy(k, i).start()
        return carry

    lax.fori_loop(1, NI, c_start, 0)

    def ag_copy(it, k, source):
        return pltpu.make_async_remote_copy(
            src_ref=crow.at[it],
            dst_ref=gath.at[it, pl.ds(source * BLK, BLK)],
            send_sem=ag_s.at[it, k], recv_sem=ag_r.at[it, k],
            device_id=(i, lax.rem(j + k, NJ)), device_id_type=MESH)

    def rs_copy(it, k, source):
        to = lax.rem(i + k, NI)
        return pltpu.make_async_remote_copy(
            src_ref=part.at[it, pl.ds(to * BLK, BLK)],
            dst_ref=recv.at[it, source],
            send_sem=rs_s.at[it, k], recv_sem=rs_r.at[it, k],
            device_id=(to, j), device_id_type=MESH)

    for dx, dy in AROUND:
        edge_here = ~there(dx, dy)

        @pl.when(edge_here)
        def _():
            xs = {-1: (0, 3), 0: (3, 16), 1: (19, 3)}[dx]
            ys = {-1: (0, 8), 0: (8, 16), 1: (24, 8)}[dy]
            sig[pl.ds(*xs), pl.ds(*ys)] = jnp.zeros((xs[1], ys[1], 16), F32)
            for it in range(ITERS):
                xr = {-1: (0, 2), 0: (2, B), 1: (B + 2, 2)}[dx]
                yr = {-1: (0, 2), 0: (2, B), 1: (B + 2, 2)}[dy]

                def zero_r(n, carry):
                    rr[it, xr[0] + n // yr[1], yr[0] + n % yr[1]] = jnp.zeros((2, 8, F), F32)
                    return carry

                lax.fori_loop(0, xr[1] * yr[1], zero_r, 0)
            if dx == 0 or dy == 0:
                xr = {-1: 0, 0: 1, 1: B + 1}[dx]
                yr = {-1: 0, 0: 1, 1: B + 1}[dy]

                def zero_v(n, carry):
                    at = (xr if dx else xr + n, yr if dy else yr + n)
                    v_nat[at[0], at[1]] = jnp.zeros((16, F), F32)
                    for it in range(ITERS):
                        cc[it, at[0], at[1]] = jnp.zeros((2, 8, F), F32)
                    return carry

                lax.fori_loop(0, B, zero_v, 0)

    def zero_ring(n, carry):
        zero = jnp.zeros((2, 8, F), F32)
        bb[0, n] = zero
        bb[E2 + 1, n] = zero
        bb[n, 0] = zero
        bb[n, E2 + 1] = zero
        return carry

    lax.fori_loop(0, E2 + 2, zero_ring, 0)

    def zero_ya(n, carry):
        zero = jnp.zeros((2, 8, F), F32)
        e_a[n, 0] = zero
        e_a[n, E2 + 1] = zero
        return carry

    def zero_faces(n, carry):
        zero = jnp.zeros((2, 8, F), F32)
        kx[E2, n] = zero
        ky[n, E2] = zero
        return carry

    lax.fori_loop(0, E2, zero_faces, 0)

    lax.fori_loop(0, E2 + 2, zero_ya, 0)

    own_s.wait()
    halo(AROUND, sig_copy, "here")

    def spread(x, carry):
        sig_t[...] = jnp.transpose(sig[x])
        for p in range(2):
            rows = sig_t[pl.ds(p, 8, stride=2), :]
            for y in range(E2 + 2):
                sig_b[x, y, p] = jnp.broadcast_to(rows[:, y + 5 : y + 6], (8, F))
        return carry

    lax.fori_loop(0, E2 + 2, spread, 0)

    level = lax.broadcasted_iota(jnp.int32, (8, F), 0)

    def faces(x0, y0):
        s = reader(sig_b, x0, y0, 1, 1)
        for x in range(2):
            for y in range(4):
                at = (x0 + x, y0 + y)
                even, odd = s(x, y, 0), s(x, y, 1)
                kz_in = 0.5 * (even + odd)
                next_even = jnp.where(level < 7, pltpu.roll(even, 7, 0), 0.0)
                bottom = 0.5 * (odd + next_even)
                kz_out = jnp.where(level < 7, bottom, 0.0)
                kz[at[0], at[1], 0] = kz_in
                kz[at[0], at[1], 1] = kz_out
                above = pltpu.roll(kz_out, 1, 0)
                for p in range(2):
                    west = 0.5 * (s(x, y, p) + s(x - 1, y, p))
                    east = 0.5 * (s(x, y, p) + s(x + 1, y, p))
                    south = 0.5 * (s(x, y, p) + s(x, y - 1, p))
                    north = 0.5 * (s(x, y, p) + s(x, y + 1, p))
                    depth = (kz_in + above) if p == 0 else (kz_in + bottom)
                    d = west + east + south + north + depth
                    kx[at[0], at[1], p] = west
                    ky[at[0], at[1], p] = south
                    dg[at[0], at[1], p] = d
                    st[at[0], at[1], p] = jnp.where(s(x, y, p) > 0.0, OMEGA / jnp.maximum(d, 1e-30), 0.0)

    blocks(0, E2, 0, E2, 2, 4, faces)

    own_v.wait()

    def permute(x, y):
        for p in range(2):
            v_per[x, y, p] = v_nat[x, y, pl.ds(p, 8, stride=2), :]

    def permute_own(n, carry):
        for y in range(B):
            permute(1 + n, 1 + y)
        return carry

    lax.fori_loop(0, B, permute_own, 0)
    halo(SIDES, v_copy, "here")

    def permute_rim(n, carry):
        permute(0, 1 + n)
        permute(B + 1, 1 + n)
        permute(1 + n, 0)
        permute(1 + n, B + 1)
        return carry

    lax.fori_loop(0, B, permute_rim, 0)

    cell = (i * B) * (NJ * B) + j * B
    source = elec_ref[0:1, :]
    sink = elec_ref[1:2, :]

    def first_residual(x0, y0):
        e = reader(v_per, x0, y0, 1, 1)
        fx, fy, fz = (reader(k, x0, y0, 2, 2) for k in (kx, ky, kz))
        for x in range(2):
            for y in range(4):
                here = cell + (x0 + x) * (NJ * B) + (y0 + y)
                force = jnp.where(source == here, CURRENT, 0.0) - jnp.where(sink == here, CURRENT, 0.0)
                force = jnp.where(level == 0, jnp.broadcast_to(force, (8, F)), 0.0)
                for p in range(2):
                    flow = stencil(e, fx, fy, fz, x, y, p, None) - dg[x0 + x + 2, y0 + y + 2, p] * e(x, y, p)
                    rr[0, x0 + x + 2, y0 + y + 2, p] = flow + force if p == 0 else flow

    blocks(0, B, 0, B, 2, 4, first_residual)

    for it in range(ITERS):
        halo(AROUND, r_copy(it), "start")

        def restrict(n, carry):
            a, b = n // 4, n % 4

            def add(x, total):
                for y in range(4):
                    for p in range(2):
                        total = total + rr[it, 2 + 4 * a + x, 2 + 4 * b + y, p]
                return total

            acc[pl.ds(pl.multiple_of(n * 8, 8), 8), :] = lax.fori_loop(0, 4, add, jnp.zeros((8, F), F32))
            return carry

        lax.fori_loop(0, 16, restrict, 0)
        rows = acc[pl.ds(0, BLK, stride=4), :]
        for q in range(1, 4):
            rows = rows + acc[pl.ds(q, BLK, stride=4), :]
        crow[it] = rows
        gath[it, pl.ds(pl.multiple_of(j * BLK, BLK), BLK)] = rows

        def ag_start(k, carry):
            ag_copy(it, k, j).start()
            return carry

        lax.fori_loop(1, NJ, ag_start, 0)

        if it == 0:
            own_c.wait()

            def c_wait(k, carry):
                c_copy(k, lax.rem(i - k + NI, NI)).wait_recv()
                return carry

            lax.fori_loop(1, NI, c_wait, 0)

        def ag_wait(k, carry):
            ag_copy(it, k, lax.rem(j - k + NJ, NJ)).wait_recv()
            return carry

        lax.fori_loop(1, NJ, ag_wait, 0)
        part[it] = jnp.dot(
            cblk[...], gath[it], precision=lax.Precision.HIGHEST, preferred_element_type=F32
        )

        def rs_start(k, carry):
            rs_copy(it, k, i).start()
            return carry

        lax.fori_loop(1, NI, rs_start, 0)

        halo(AROUND, r_copy(it), "here")

        def first_sweep(x0, y0):
            for x in range(2):
                for y in range(4):
                    for p in range(2):
                        bb[x0 + x + 1, y0 + y + 1, p] = st[x0 + x, y0 + y, p] * rr[it, x0 + x, y0 + y, p]

        blocks(0, E2, 0, E2, 2, 4, first_sweep)

        def sweep(src, store):
            def body(x0, y0):
                e = reader(src, x0, y0, 1, 1)
                fx, fy, fz = (reader(k, x0, y0, 0, 0) for k in (kx, ky, kz))
                for x in range(2):
                    for y in range(4):
                        for p in range(2):
                            nearby = stencil(e, fx, fy, fz, x, y, p, None)
                            value = ((1.0 - OMEGA) * e(x, y, p) + bb[x0 + x + 1, y0 + y + 1, p]
                                     + st[x0 + x, y0 + y, p] * nearby)
                            store(x0 + x, y0 + y, p, value)
            return body

        def into_a(x, y, p, value):
            e_a[x + 1, y + 1, p] = value

        def into_b(x, y, p, value):
            e_b[x + 1, y + 1, p] = value

        blocks(0, E2, 0, E2, 2, 4, sweep(bb, into_a))
        blocks(1, B + 2, 0, E2, 2, 4, sweep(e_a, into_b))

        def rs_wait(k, carry):
            rs_copy(it, k, lax.rem(i - k + NI, NI)).wait_recv()
            return carry

        lax.fori_loop(1, NI, rs_wait, 0)
        recv[it, i] = part[it, pl.ds(pl.multiple_of(i * BLK, BLK), BLK)]
        total = recv[it, 0]
        for q in range(1, NI):
            total = total + recv[it, q]
        for q in range(4):
            pro[pl.ds(q, BLK, stride=4), :] = total

        def correct(x0, y0):
            e = reader(e_b, x0, y0, 1, 1)
            fx, fy, fz = (reader(k, x0, y0, 0, 0) for k in (kx, ky, kz))
            block = ((x0 - 2) // 4) * 4 + (y0 - 2) // 4
            coarse = pro[pl.ds(pl.multiple_of(block * 8, 8), 8), :]
            for x in range(2):
                for y in range(4):
                    for p in range(2):
                        nearby = stencil(e, fx, fy, fz, x, y, p, None)
                        value = ((1.0 - OMEGA) * e(x, y, p) + bb[x0 + x + 1, y0 + y + 1, p]
                                 + st[x0 + x, y0 + y, p] * nearby) + coarse
                        cc[it, x0 + x - 1, y0 + y - 1, p] = value
                        v_per[x0 + x - 1, y0 + y - 1, p] = v_per[x0 + x - 1, y0 + y - 1, p] + value

        blocks(2, B, 2, B, 2, 4, correct)
        halo(SIDES, h_copy(it), "start")

        if it + 1 == ITERS:
            def unpermute(n, carry):
                for y in range(B):
                    for p in range(2):
                        v_nat[1 + n, 1 + y, pl.ds(p, 8, stride=2), :] = v_per[1 + n, 1 + y, p]
                return carry

            lax.fori_loop(0, B, unpermute, 0)
            out_v = pltpu.make_async_copy(v_nat.at[pl.ds(1, B), pl.ds(1, B)], pot_hbm, loc.at[0])
            out_v.start()

        halo(SIDES, h_copy(it), "here")

        def update(x0, y0):
            e = reader(cc.at[it], x0, y0, 1, 1)
            fx, fy, fz = (reader(k, x0, y0, 2, 2) for k in (kx, ky, kz))
            for x in range(2):
                for y in range(4):
                    for p in range(2):
                        flow = stencil(e, fx, fy, fz, x, y, p, None) - dg[x0 + x + 2, y0 + y + 2, p] * e(x, y, p)
                        value = rr[it, x0 + x + 2, y0 + y + 2, p] + flow
                        if it + 1 < ITERS:
                            rr[it + 1, x0 + x + 2, y0 + y + 2, p] = value
                        else:
                            res_nat[x0 + x, y0 + y, pl.ds(p, 8, stride=2), :] = value

        blocks(0, B, 0, B, 2, 4, update)

    out_r = pltpu.make_async_copy(res_nat, res_hbm, loc.at[1])
    out_r.start()
    out_v.wait()
    out_r.wait()

    halo(AROUND, sig_copy, "sent")
    halo(SIDES, v_copy, "sent")

    def c_sent(k, carry):
        c_copy(k, i).wait_send()
        return carry

    lax.fori_loop(1, NI, c_sent, 0)
    for it in range(ITERS):
        halo(AROUND, r_copy(it), "sent")
        halo(SIDES, h_copy(it), "sent")

        def ag_sent(k, carry):
            ag_copy(it, k, j).wait_send()
            return carry

        lax.fori_loop(1, NJ, ag_sent, 0)

        def rs_sent(k, carry):
            rs_copy(it, k, i).wait_send()
            return carry

        lax.fori_loop(1, NI, rs_sent, 0)


def on_device(start_potentials, conductivity, electrodes, coarse_inverse):
    shape = jax.ShapeDtypeStruct((B, B, B, F), F32)
    tiles = lambda *lead: pltpu.VMEM(tuple(lead) + (2, 8, F), F32)
    dma = pltpu.SemaphoreType.DMA
    anywhere = pl.BlockSpec(memory_space=pl.ANY)
    return pl.pallas_call(
        kernel,
        out_shape=(shape, shape),
        in_specs=[anywhere, anywhere, pl.BlockSpec(memory_space=pltpu.VMEM), anywhere],
        out_specs=(anywhere, anywhere),
        scratch_shapes=[
            pltpu.VMEM((22, 32, 16), F32),
            pltpu.VMEM((16, 32), F32),
            tiles(22, 22),
            pltpu.VMEM((18, 18, 16, F), F32),
            tiles(18, 18),
            tiles(ITERS, 20, 20),
            tiles(22, 22),
            tiles(22, 22),
            tiles(22, 22),
            tiles(ITERS, 18, 18),
            tiles(21, 20),
            tiles(20, 21),
            tiles(20, 20),
            tiles(20, 20),
            tiles(20, 20),
            pltpu.VMEM((16, 16, 16, F), F32),
            pltpu.VMEM((256, 512), F32),
            pltpu.VMEM((ITERS, BLK, F), F32),
            pltpu.VMEM((ITERS, 512, F), F32),
            pltpu.VMEM((ITERS, 256, F), F32),
            pltpu.VMEM((ITERS, NI, BLK, F), F32),
            pltpu.VMEM((128, F), F32),
            pltpu.VMEM((128, F), F32),
            dma((8,)), dma((8,)),
            dma((4,)), dma((4,)),
            dma((NI,)), dma((NI,)),
            dma((ITERS, NJ)), dma((ITERS, NJ)),
            dma((ITERS, NI)), dma((ITERS, NI)),
            dma((ITERS, 8)), dma((ITERS, 8)),
            dma((ITERS, 4)), dma((ITERS, 4)),
            dma((3,)),
        ],
        compiler_params=pltpu.CompilerParams(
            collective_id=0, has_side_effects=True, vmem_limit_bytes=60 * 2**20
        ),
        cost_estimate=pl.CostEstimate(flops=10**8, bytes_accessed=10**7, transcendentals=0),
    )(start_potentials, conductivity, electrodes.T, coarse_inverse)


def solution(mesh):
    in_specs = (P("gx", "gy", None, None), P("gx", "gy", None), P(), P(("gx", "gy"), None))
    out_specs = (P("gx", "gy", None, None), P("gx", "gy", None, None))
    return jax.shard_map(
        on_device, mesh=mesh, in_specs=in_specs, out_specs=out_specs, check_vma=False
    )
```

```python
import jax
import jax.numpy as jnp
from jax import lax
from jax.experimental import pallas as pl
from jax.experimental.pallas import tpu as pltpu
from jax.sharding import PartitionSpec as P

OMEGA = 0.7
CURRENT = 8.0
ITERS = 2
NI, NJ = 8, 16
NQ = NJ // 2
B = 16
F = 128
E2 = B + 4
BLK = 32
MESH = pl.DeviceIdType.MESH
F32 = jnp.float32

SIDES = ((-1, 0), (1, 0), (0, -1), (0, 1))
CORNERS = ((-1, -1), (-1, 1), (1, -1), (1, 1))
AROUND = SIDES + CORNERS


def stencil(e, kx, ky, kz, x, y, p):
    total = kx(x, y, p) * e(x - 1, y, p) + kx(x + 1, y, p) * e(x + 1, y, p)
    total = total + (ky(x, y, p) * e(x, y - 1, p) + ky(x, y + 1, p) * e(x, y + 1, p))
    other = e(x, y, 1 - p)
    if p == 0:
        across = pltpu.roll(kz(x, y, 1) * other, 1, 0)
    else:
        across = kz(x, y, 1) * pltpu.roll(other, 7, 0)
    return total + (kz(x, y, 0) * other + across)


def reader(ref, x0, y0, shift):
    held = {}

    def get(x, y, p):
        key = (x, y, p)
        if key not in held:
            held[key] = ref[x0 + (x + shift), y0 + (y + shift), p]
        return held[key]

    return get


def region(body, x_lo, x_n, y_lo, y_n, xb, yb, copies=1, step_x=0, step_y=0):
    nx, ny = x_n // xb, y_n // yb
    assert nx * xb == x_n and ny * yb == y_n
    cells = [(x, y, p) for x in range(xb) for y in range(yb) for p in range(2)]

    def one(n, carry):
        x0, y0 = x_lo, y_lo
        if copies > 1:
            side = n // (nx * ny)
            x0, y0 = x0 + side * step_x, y0 + side * step_y
            n = n % (nx * ny) if nx * ny > 1 else 0
        if nx > 1:
            x0 = x0 + (n // ny) * xb
        if ny > 1:
            y0 = y0 + ((n % ny) if nx > 1 else n) * yb
        body(x0, y0, cells)
        return carry

    lax.fori_loop(0, copies * nx * ny, one, 0)


def kernel(
    v_hbm, cond_ref, elec_ref, cinv_hbm,
    pot_hbm, res_hbm,
    sig, sig_t, v_nat, uu, rr, bb, e_a, e_b, kx, ky, kz, st, dg, res_nat,
    cblk, crow, gath, part, recv, pro, acc,
    sig_s, sig_r, u_s, u_r, c_s, c_r, ag_s, ag_r, tw_s, tw_r, rs_s, rs_r, loc,
):
    i = lax.axis_index("gx")
    j = lax.axis_index("gy")
    core = lax.rem(j, 2)
    pair = j // 2
    sig_b = uu.at[ITERS]

    def there(dx, dy):
        ok = None
        for d, pos, n in ((dx, i, NI), (dy, j, NJ)):
            if d:
                term = (pos > 0) if d < 0 else (pos < n - 1)
                ok = term if ok is None else ok & term
        return ok

    bar = pltpu.get_barrier_semaphore()

    def greet(to_i, to_j):
        pl.semaphore_signal(bar, inc=1, device_id=(to_i, to_j), device_id_type=MESH)

    count = jnp.int32(NI - 1 + NQ - 1)
    for dx, dy in ((0, -1), (0, 1)) + CORNERS:
        ok = there(dx, dy)

        @pl.when(ok)
        def _():
            greet(i + dx, j + dy)

        count = count + jnp.where(ok, 1, 0)

    def greet_j(k, carry):
        greet(i, lax.rem(j + 2 * k, NJ))
        return carry

    def greet_i(k, carry):
        greet(lax.rem(i + k, NI), j)
        return carry

    lax.fori_loop(1, NQ, greet_j, 0)
    lax.fori_loop(1, NI, greet_i, 0)

    own_s = pltpu.make_async_copy(cond_ref, sig.at[pl.ds(3, B), pl.ds(8, B)], loc.at[2])
    own_s.start()
    own_v = pltpu.make_async_copy(v_hbm, v_nat, loc.at[0])
    own_v.start()
    own_c = pltpu.make_async_copy(
        cinv_hbm.at[:, pl.ds(i * 512, 512)], cblk.at[pl.ds(i * BLK, BLK)], loc.at[1]
    )
    own_c.start()

    def halo(dirs, make, what):
        for n, (dx, dy) in enumerate(dirs):
            if what in ("start", "sent"):

                @pl.when(there(dx, dy))
                def _():
                    copy = make(n, dx, dy)
                    copy.start() if what == "start" else copy.wait_send()

            else:

                @pl.when(there(-dx, -dy))
                def _():
                    make(n, dx, dy).wait_recv()

    def sig_copy(n, dx, dy):
        xs = {-1: (3, 3, 19), 0: (3, 16, 3), 1: (16, 3, 0)}[dx]
        ys = {-1: (8, 8, 24), 0: (8, 16, 8), 1: (16, 8, 0)}[dy]
        src = cond_ref.at[pl.ds(xs[0] - 3, xs[1]), pl.ds(ys[0] - 8, ys[1])]
        dst = sig.at[pl.ds(xs[2], xs[1]), pl.ds(ys[2], ys[1])]
        return pltpu.make_async_remote_copy(
            src_ref=src, dst_ref=dst, send_sem=sig_s.at[n], recv_sem=sig_r.at[n],
            device_id=(i + dx, j + dy), device_id_type=MESH)

    def u_copy(level, base, x_layers, y_layers):
        def span(d, layers):
            if d == 0:
                return 3, B, 3
            first, number = layers
            start = 3 + first if d < 0 else 3 + B - first - number
            return start, number, start - d * B

        def make(n, dx, dy):
            xs, ys = span(dx, x_layers), span(dy, y_layers)
            return pltpu.make_async_remote_copy(
                src_ref=uu.at[level, pl.ds(xs[0], xs[1]), pl.ds(ys[0], ys[1])],
                dst_ref=uu.at[level, pl.ds(xs[2], xs[1]), pl.ds(ys[2], ys[1])],
                send_sem=u_s.at[level, base + n], recv_sem=u_r.at[level, base + n],
                device_id=(i + dx, j + dy), device_id_type=MESH)

        return make

    def near(level, what):
        halo(SIDES, u_copy(level, 0, (0, 1), (0, 1)), what)

    def far(level, what):
        halo(SIDES, u_copy(level, 4, (1, 2), (1, 2)), what)
        halo(CORNERS, u_copy(level, 8, (0, 2), (0, 3)), what)
        halo(CORNERS, u_copy(level, 12, (2, 1), (0, 1)), what)

    def c_copy(k, source):
        to = lax.rem(i + k, NI)
        return pltpu.make_async_remote_copy(
            src_ref=cinv_hbm.at[:, pl.ds(to * 512, 512)],
            dst_ref=cblk.at[pl.ds(source * BLK, BLK)],
            send_sem=c_s.at[k], recv_sem=c_r.at[k],
            device_id=(to, j), device_id_type=MESH)

    def ag_copy(it, k, source):
        return pltpu.make_async_remote_copy(
            src_ref=crow.at[it],
            dst_ref=gath.at[it, source, core],
            send_sem=ag_s.at[it, k], recv_sem=ag_r.at[it, k],
            device_id=(i, lax.rem(j + 2 * k, NJ)), device_id_type=MESH)

    def twin_copy(it, which):
        return pltpu.make_async_remote_copy(
            src_ref=gath.at[it, :, which], dst_ref=gath.at[it, :, which],
            send_sem=tw_s.at[it], recv_sem=tw_r.at[it],
            device_id=(i, j + 1 - 2 * core), device_id_type=MESH)

    def rs_copy(it, k, source):
        to = lax.rem(i + k, NI)
        return pltpu.make_async_remote_copy(
            src_ref=part.at[it, pl.ds(to * BLK, BLK)],
            dst_ref=recv.at[it, source],
            send_sem=rs_s.at[it, k], recv_sem=rs_r.at[it, k],
            device_id=(to, j), device_id_type=MESH)

    for dx, dy in AROUND:

        @pl.when(~there(dx, dy))
        def _():
            xs = {-1: (0, 3), 0: (3, 16), 1: (19, 3)}[dx]
            ys = {-1: (0, 8), 0: (8, 16), 1: (24, 8)}[dy]
            sig[pl.ds(*xs), pl.ds(*ys)] = jnp.zeros((xs[1], ys[1], 16), F32)

    def spread(columns, copies, inner):
        def one(n, carry):
            x = copies[0] + n + (n // copies[1]) * copies[2]
            if inner:
                sig_t[:, 8 : 8 + B] = jnp.transpose(sig[x, 8 : 8 + B])
            else:
                sig_t[...] = jnp.transpose(sig[x])
            for p in range(2):
                rows = sig_t[pl.ds(p, 8, stride=2), :]
                for y in columns:
                    sig_b[x, y, p] = jnp.broadcast_to(rows[:, y + 5 : y + 6], (8, F))
            return carry

        return one

    own_s.wait()
    lax.fori_loop(0, B, spread(range(3, 3 + B), (3, B, 0), True), 0)

    level = lax.broadcasted_iota(jnp.int32, (8, F), 0)

    def faces(x0, y0, cells):
        s = reader(sig_b, x0, y0, 1)
        done = {}
        for x, y, p in cells:
            if p:
                continue
            even, odd = s(x, y, 0), s(x, y, 1)
            kz_in = 0.5 * (even + odd)
            next_even = jnp.where(level < 7, pltpu.roll(even, 7, 0), 0.0)
            bottom = 0.5 * (odd + next_even)
            kz_out = jnp.where(level < 7, bottom, 0.0)
            above = pltpu.roll(kz_out, 1, 0)
            for q in range(2):
                west = 0.5 * (s(x, y, q) + s(x - 1, y, q))
                east = 0.5 * (s(x, y, q) + s(x + 1, y, q))
                south = 0.5 * (s(x, y, q) + s(x, y - 1, q))
                north = 0.5 * (s(x, y, q) + s(x, y + 1, q))
                depth = (kz_in + above) if q == 0 else (kz_in + bottom)
                d = west + east + south + north + depth
                step = jnp.where(s(x, y, q) > 0.0, OMEGA / jnp.maximum(d, 1e-30), 0.0)
                done[x, y, q] = west, south, (kz_in, kz_out)[q], d, step
        for (x, y, p), values in done.items():
            for ref, value in zip((kx, ky, kz, dg, st), values):
                ref[x0 + x, y0 + y, p] = value

    region(faces, 3, 14, 3, 14, 7, 2)

    own_v.wait()

    def permute(n, carry):
        for y in range(B):
            for p in range(2):
                uu[0, 3 + n, 3 + y, p] = v_nat[n, y, pl.ds(p, 8, stride=2), :]
        return carry

    lax.fori_loop(0, B, permute, 0)

    pl.semaphore_wait(bar, count)
    halo(AROUND, sig_copy, "start")
    near(0, "start")
    far(0, "start")

    def c_start(k, carry):
        c_copy(k, i).start()
        return carry

    lax.fori_loop(1, NI, c_start, 0)

    for dx, dy in AROUND:

        @pl.when(~there(dx, dy))
        def _():
            xr = {-1: (0, 3), 0: (3, B), 1: (B + 3, 3)}[dx]
            yr = {-1: (0, 3), 0: (3, B), 1: (B + 3, 3)}[dy]

            def zero_u(n, carry):
                for w in range(ITERS):
                    uu[w, xr[0] + n // yr[1], yr[0] + n % yr[1]] = jnp.zeros((2, 8, F), F32)
                return carry

            lax.fori_loop(0, xr[1] * yr[1], zero_u, 0)

    def zero_ring(n, carry):
        zero = jnp.zeros((2, 8, F), F32)
        bb[0, n] = zero
        bb[E2 + 1, n] = zero
        bb[n, 0] = zero
        bb[n, E2 + 1] = zero
        return carry

    lax.fori_loop(0, E2 + 2, zero_ring, 0)

    corner = (i * B - 2) * (NJ * B) + (j * B - 2)
    source = elec_ref[0:1, :]
    sink = elec_ref[1:2, :]

    def residual(n):
        def body(x0, y0, cells):
            e = reader(uu.at[n], x0, y0, 1)
            fx, fy, fz = (reader(k, x0, y0, 0) for k in (kx, ky, kz))
            done = {}
            for x, y, p in cells:
                value = stencil(e, fx, fy, fz, x, y, p) - dg[x0 + x, y0 + y, p] * e(x, y, p)
                if n > 0:
                    value = rr[x0 + x, y0 + y, p] + value
                elif p == 0:
                    here = corner + (x0 + x) * (NJ * B) + (y0 + y)
                    force = jnp.where(source == here, CURRENT, 0.0) - jnp.where(sink == here, CURRENT, 0.0)
                    value = value + jnp.where(level == 0, jnp.broadcast_to(force, (8, F)), 0.0)
                done[x, y, p] = value, (st[x0 + x, y0 + y, p] * value if n < ITERS else None)
            for (x, y, p), (value, first) in done.items():
                if n < ITERS:
                    rr[x0 + x, y0 + y, p] = value
                    bb[x0 + x + 1, y0 + y + 1, p] = first
                else:
                    res_nat[x0 + x - 2, y0 + y - 2, pl.ds(p, 8, stride=2), :] = value

        return body

    def residual_own_rim(n):
        region(residual(n), 2, 1, 2, 16, 1, 16, 2, 15, 0)
        region(residual(n), 3, 14, 2, 1, 14, 1, 2, 0, 15)

    halo(AROUND, sig_copy, "here")
    lax.fori_loop(0, 6, spread(range(E2 + 2), (0, 3, 16), False), 0)
    lax.fori_loop(0, B, spread((0, 1, 2, 19, 20, 21), (3, B, 0), False), 0)
    region(faces, 0, 3, 0, 20, 3, 10, 2, 17, 0)
    region(faces, 3, 14, 0, 3, 7, 3, 2, 0, 17)

    def last_faces(n, carry):
        for p in range(2):
            kx[E2, n, p] = 0.5 * (sig_b[E2 + 1, n + 1, p] + sig_b[E2, n + 1, p])
            ky[n, E2, p] = 0.5 * (sig_b[n + 1, E2 + 1, p] + sig_b[n + 1, E2, p])
        return carry

    lax.fori_loop(0, E2, last_faces, 0)

    for dx, dy in SIDES:

        @pl.when(~there(dx, dy))
        def _():
            def zero_last(n, carry):
                x = {-1: 2, 0: 3 + n, 1: B + 3}[dx]
                y = {-1: 2, 0: 3 + n, 1: B + 3}[dy]
                uu[ITERS, x, y] = jnp.zeros((2, 8, F), F32)
                return carry

            lax.fori_loop(0, B, zero_last, 0)

    def sweep(src, shift, store):
        def body(x0, y0, cells):
            e = reader(src, x0, y0, shift)
            fx, fy, fz = (reader(k, x0, y0, 0) for k in (kx, ky, kz))
            done = {}
            for x, y, p in cells:
                nearby = stencil(e, fx, fy, fz, x, y, p)
                done[x, y, p] = ((1.0 - OMEGA) * e(x, y, p) + bb[x0 + x + 1, y0 + y + 1, p]
                                 + st[x0 + x, y0 + y, p] * nearby)
            for (x, y, p), value in done.items():
                store(x0 + x, y0 + y, p, value)

        return body

    def into_a(x, y, p, value):
        e_a[x, y, p] = value

    def into_b(x, y, p, value):
        e_b[x, y, p] = value

    def coarse_at(x, y):
        block = ((x - 2) // 4) * 4 + (y - 2) // 4
        return pro[pl.ds(pl.multiple_of(block * 8, 8), 8), :]

    for it in range(ITERS):
        region(residual(it), 3, 14, 3, 14, 7, 2)
        near(it, "here")
        residual_own_rim(it)

        def restrict(n, carry):
            a, b = n // 4, n % 4
            tiles = [rr[2 + 4 * a + x, 2 + 4 * b + y, p] for x in range(4) for y in range(4) for p in range(2)]
            while len(tiles) > 1:
                tiles = [one + two for one, two in zip(tiles[::2], tiles[1::2])]
            acc[pl.ds(pl.multiple_of(n * 8, 8), 8), :] = tiles[0]
            return carry

        lax.fori_loop(0, 16, restrict, 0)
        rows = acc[pl.ds(0, BLK, stride=4), :]
        for q in range(1, 4):
            rows = rows + acc[pl.ds(q, BLK, stride=4), :]
        crow[it] = rows
        gath[it, pair, core] = rows

        def ag_start(k, carry):
            ag_copy(it, k, pair).start()
            return carry

        lax.fori_loop(1, NQ, ag_start, 0)

        region(sweep(bb, 1, into_a), 3, 14, 3, 14, 7, 2)
        region(sweep(e_a, 0, into_b), 4, 12, 4, 12, 6, 3)

        def ag_wait(k, carry):
            ag_copy(it, k, lax.rem(pair - k + NQ, NQ)).wait_recv()
            return carry

        lax.fori_loop(1, NQ, ag_wait, 0)
        twin_copy(it, core).start()

        def into_u(x, y, p, value):
            uu[it + 1, x + 1, y + 1, p] = value

        region(sweep(e_b, 0, into_u), 5, 10, 5, 10, 5, 5)

        if it == 0:
            own_c.wait()

            def c_wait(k, carry):
                c_copy(k, lax.rem(i - k + NI, NI)).wait_recv()
                return carry

            lax.fori_loop(1, NI, c_wait, 0)

        twin_copy(it, 1 - core).wait_recv()
        part[it] = jnp.dot(
            cblk[...], gath[it].reshape(512, F), precision=lax.Precision.HIGHEST, preferred_element_type=F32
        )

        def rs_start(k, carry):
            rs_copy(it, k, i).start()
            return carry

        lax.fori_loop(1, NI, rs_start, 0)

        far(it, "here")
        region(residual(it), 0, 2, 0, 20, 2, 10, 2, 18, 0)
        region(residual(it), 2, 16, 0, 2, 8, 2, 2, 0, 18)
        region(sweep(bb, 1, into_a), 0, 3, 0, 20, 3, 10, 2, 17, 0)
        region(sweep(bb, 1, into_a), 3, 14, 0, 3, 7, 3, 2, 0, 17)
        region(sweep(e_a, 0, into_b), 1, 3, 1, 18, 3, 9, 2, 15, 0)
        region(sweep(e_a, 0, into_b), 4, 12, 1, 3, 6, 3, 2, 0, 15)

        def rs_wait(k, carry):
            rs_copy(it, k, lax.rem(i - k + NI, NI)).wait_recv()
            return carry

        lax.fori_loop(1, NI, rs_wait, 0)
        recv[it, i] = part[it, pl.ds(pl.multiple_of(i * BLK, BLK), BLK)]
        total = recv[it, 0]
        for q in range(1, NI):
            total = total + recv[it, q]
        for q in range(4):
            pro[pl.ds(q, BLK, stride=4), :] = total

        def into_u_coarse(x, y, p, value):
            uu[it + 1, x + 1, y + 1, p] = value + coarse_at(x, y)

        region(sweep(e_b, 0, into_u_coarse), 2, 3, 2, 16, 3, 8, 2, 13, 0)
        region(sweep(e_b, 0, into_u_coarse), 5, 10, 2, 3, 10, 3, 2, 0, 13)
        near(it + 1, "start")
        if it + 1 < ITERS:
            far(it + 1, "start")

        def add_coarse(x0, y0, cells):
            done = {}
            for x, y, p in cells:
                done[x, y, p] = uu[it + 1, x0 + x + 1, y0 + y + 1, p] + coarse_at(x0 + x, y0 + y)
            for (x, y, p), value in done.items():
                uu[it + 1, x0 + x + 1, y0 + y + 1, p] = value

        region(add_coarse, 5, 10, 5, 10, 5, 2)

    def potentials(x0, y0, cells):
        done = {}
        for x, y, p in cells:
            total = uu[0, x0 + x + 1, y0 + y + 1, p]
            for n in range(ITERS):
                total = total + uu[n + 1, x0 + x + 1, y0 + y + 1, p]
            done[x, y, p] = total
        for (x, y, p), value in done.items():
            v_nat[x0 + x - 2, y0 + y - 2, pl.ds(p, 8, stride=2), :] = value

    region(potentials, 2, B, 2, B, 4, 4)
    out_v = pltpu.make_async_copy(v_nat, pot_hbm, loc.at[0])
    out_v.start()
    region(residual(ITERS), 3, 14, 3, 14, 7, 2)
    near(ITERS, "here")
    residual_own_rim(ITERS)
    out_r = pltpu.make_async_copy(res_nat, res_hbm, loc.at[1])
    out_r.start()
    out_v.wait()

    halo(AROUND, sig_copy, "sent")

    def c_sent(k, carry):
        c_copy(k, i).wait_send()
        return carry

    lax.fori_loop(1, NI, c_sent, 0)
    near(ITERS, "sent")
    for it in range(ITERS):
        near(it, "sent")
        far(it, "sent")
        twin_copy(it, core).wait_send()

        def ag_sent(k, carry):
            ag_copy(it, k, pair).wait_send()
            return carry

        lax.fori_loop(1, NQ, ag_sent, 0)

        def rs_sent(k, carry):
            rs_copy(it, k, i).wait_send()
            return carry

        lax.fori_loop(1, NI, rs_sent, 0)
    out_r.wait()


def on_device(start_potentials, conductivity, electrodes, coarse_inverse):
    shape = jax.ShapeDtypeStruct((B, B, B, F), F32)
    tiles = lambda *lead: pltpu.VMEM(tuple(lead) + (2, 8, F), F32)
    dma = pltpu.SemaphoreType.DMA
    anywhere = pl.BlockSpec(memory_space=pl.ANY)
    return pl.pallas_call(
        kernel,
        out_shape=(shape, shape),
        in_specs=[anywhere, anywhere, pl.BlockSpec(memory_space=pltpu.VMEM), anywhere],
        out_specs=(anywhere, anywhere),
        scratch_shapes=[
            pltpu.VMEM((22, 32, 16), F32),
            pltpu.VMEM((16, 32), F32),
            pltpu.VMEM((B, B, 16, F), F32),
            tiles(ITERS + 1, 22, 22),
            tiles(20, 20),
            tiles(22, 22),
            tiles(20, 20),
            tiles(20, 20),
            tiles(21, 20),
            tiles(20, 21),
            tiles(20, 20),
            tiles(20, 20),
            tiles(20, 20),
            pltpu.VMEM((B, B, 16, F), F32),
            pltpu.VMEM((256, 512), F32),
            pltpu.VMEM((ITERS, BLK, F), F32),
            pltpu.VMEM((ITERS, NQ, 2, BLK, F), F32),
            pltpu.VMEM((ITERS, 256, F), F32),
            pltpu.VMEM((ITERS, NI, BLK, F), F32),
            pltpu.VMEM((128, F), F32),
            pltpu.VMEM((128, F), F32),
            dma((8,)), dma((8,)),
            dma((ITERS + 1, 16)), dma((ITERS + 1, 16)),
            dma((NI,)), dma((NI,)),
            dma((ITERS, NQ)), dma((ITERS, NQ)),
            dma((ITERS,)), dma((ITERS,)),
            dma((ITERS, NI)), dma((ITERS, NI)),
            dma((3,)),
        ],
        compiler_params=pltpu.CompilerParams(
            collective_id=0, has_side_effects=True, vmem_limit_bytes=56 * 2**20
        ),
        cost_estimate=pl.CostEstimate(flops=10**8, bytes_accessed=10**7, transcendentals=0),
    )(start_potentials, conductivity, electrodes.T, coarse_inverse)


def solution(mesh):
    in_specs = (P("gx", "gy", None, None), P("gx", "gy", None), P(), P(("gx", "gy"), None))
    out_specs = (P("gx", "gy", None, None), P("gx", "gy", None, None))
    return jax.shard_map(
        on_device, mesh=mesh, in_specs=in_specs, out_specs=out_specs, check_vma=False
    )
```

```python
import jax
import jax.numpy as jnp
from jax import lax
from jax.experimental import pallas as pl
from jax.experimental.pallas import tpu as pltpu
from jax.sharding import PartitionSpec as P

OMEGA = 0.7
CURRENT = 8.0
ITERS = 2
NI, NJ = 8, 16
NK, NR = 8, 16
B = 16
F = 128
E2 = B + 4
BLK = 32
MESH = pl.DeviceIdType.MESH
F32 = jnp.float32

SIDES = ((-1, 0), (1, 0), (0, -1), (0, 1))
CORNERS = ((-1, -1), (-1, 1), (1, -1), (1, 1))
AROUND = SIDES + CORNERS


def stencil(e, kx, ky, kz, x, y, p):
    total = kx(x, y, p) * e(x - 1, y, p) + kx(x + 1, y, p) * e(x + 1, y, p)
    total = total + (ky(x, y, p) * e(x, y - 1, p) + ky(x, y + 1, p) * e(x, y + 1, p))
    other = e(x, y, 1 - p)
    if p == 0:
        across = pltpu.roll(kz(x, y, 1) * other, 1, 0)
    else:
        across = kz(x, y, 1) * pltpu.roll(other, 7, 0)
    return total + (kz(x, y, 0) * other + across)


def reader(ref, x0, y0, shift):
    held = {}

    def get(x, y, p):
        key = (x, y, p)
        if key not in held:
            held[key] = ref[x0 + (x + shift), y0 + (y + shift), p]
        return held[key]

    return get


def region(body, x_lo, x_n, y_lo, y_n, xb, yb, copies=1, step_x=0, step_y=0):
    nx, ny = x_n // xb, y_n // yb
    assert nx * xb == x_n and ny * yb == y_n
    cells = [(x, y, p) for x in range(xb) for y in range(yb) for p in range(2)]

    def one(n, carry):
        x0, y0 = x_lo, y_lo
        if copies > 1:
            side = n // (nx * ny)
            x0, y0 = x0 + side * step_x, y0 + side * step_y
            n = n % (nx * ny) if nx * ny > 1 else 0
        if nx > 1:
            x0 = x0 + (n // ny) * xb
        if ny > 1:
            y0 = y0 + ((n % ny) if nx > 1 else n) * yb
        body(x0, y0, cells)
        return carry

    lax.fori_loop(0, copies * nx * ny, one, 0)


def kernel(
    v_hbm, cond_ref, elec_ref, cinv_hbm,
    v_nat, res_nat,
    sig, sig_t, uu, rr, bb, e_a, e_b, kx, ky, kz, st, dg,
    cblk, crow, gath, part, recv, pro, acc,
    sig_s, sig_r, u_s, u_r, c_s, c_r, ag_s, ag_r, rs_s, rs_r, loc,
):
    i = lax.axis_index("gx")
    j = lax.axis_index("gy")
    high, y_at = i // 4, lax.rem(i, 4)
    z_at, low = j // 4, lax.rem(j, 4)
    k_at = high * 4 + low
    r_at = y_at * 4 + z_at
    sig_b = uu.at[ITERS]

    def there(dx, dy):
        ok = None
        for d, pos, n in ((dx, i, NI), (dy, j, NJ)):
            if d:
                term = (pos > 0) if d < 0 else (pos < n - 1)
                ok = term if ok is None else ok & term
        return ok

    bar = pltpu.get_barrier_semaphore()

    def greet(to_i, to_j):
        pl.semaphore_signal(bar, inc=1, device_id=(to_i, to_j), device_id_type=MESH)

    def k_peer(k):
        to = lax.rem(k_at + k, NK)
        return to, ((to // 4) * 4 + y_at, z_at * 4 + lax.rem(to, 4))

    def r_peer(k):
        to = lax.rem(r_at + k, NR)
        return to, (high * 4 + to // 4, lax.rem(to, 4) * 4 + low)

    count = jnp.int32(NK - 1 + NR - 1)
    for dx, dy in AROUND:
        ok = there(dx, dy)
        if dy == 0:
            ok = ok & ((i + dx) // 4 != high)
        if dx == 0:
            ok = ok & ((j + dy) // 4 != z_at)

        @pl.when(ok)
        def _():
            greet(i + dx, j + dy)

        count = count + jnp.where(ok, 1, 0)

    def greet_k(k, carry):
        greet(*k_peer(k)[1])
        return carry

    def greet_r(k, carry):
        greet(*r_peer(k)[1])
        return carry

    lax.fori_loop(1, NK, greet_k, 0)
    lax.fori_loop(1, NR, greet_r, 0)

    own_s = pltpu.make_async_copy(cond_ref, sig.at[pl.ds(3, B), pl.ds(8, B)], loc.at[2])
    own_s.start()
    own_v = pltpu.make_async_copy(v_hbm, v_nat, loc.at[3])
    own_v.start()
    own_c = [
        pltpu.make_async_copy(
            cinv_hbm.at[:, pl.ds(pl.multiple_of(h * 2048 + r_at * 128, 128), 128)],
            cblk.at[pl.ds(r_at * BLK, BLK), pl.ds(h * 128, 128)],
            loc.at[h],
        )
        for h in range(2)
    ]
    for copy in own_c:
        copy.start()

    def halo(dirs, make, what):
        for n, (dx, dy) in enumerate(dirs):
            if what in ("start", "sent"):

                @pl.when(there(dx, dy))
                def _():
                    copy = make(n, dx, dy)
                    copy.start() if what == "start" else copy.wait_send()

            else:

                @pl.when(there(-dx, -dy))
                def _():
                    make(n, dx, dy).wait_recv()

    def sig_copy(n, dx, dy):
        xs = {-1: (3, 3, 19), 0: (3, 16, 3), 1: (16, 3, 0)}[dx]
        ys = {-1: (8, 8, 24), 0: (8, 16, 8), 1: (16, 8, 0)}[dy]
        src = cond_ref.at[pl.ds(xs[0] - 3, xs[1]), pl.ds(ys[0] - 8, ys[1])]
        dst = sig.at[pl.ds(xs[2], xs[1]), pl.ds(ys[2], ys[1])]
        return pltpu.make_async_remote_copy(
            src_ref=src, dst_ref=dst, send_sem=sig_s.at[n], recv_sem=sig_r.at[n],
            device_id=(i + dx, j + dy), device_id_type=MESH)

    def u_copy(level, base, x_layers, y_layers):
        def span(d, layers):
            if d == 0:
                return 3, B, 3
            first, number = layers
            start = 3 + first if d < 0 else 3 + B - first - number
            return start, number, start - d * B

        def make(n, dx, dy):
            xs, ys = span(dx, x_layers), span(dy, y_layers)
            return pltpu.make_async_remote_copy(
                src_ref=uu.at[level, pl.ds(xs[0], xs[1]), pl.ds(ys[0], ys[1])],
                dst_ref=uu.at[level, pl.ds(xs[2], xs[1]), pl.ds(ys[2], ys[1])],
                send_sem=u_s.at[level, base + n], recv_sem=u_r.at[level, base + n],
                device_id=(i + dx, j + dy), device_id_type=MESH)

        return make

    def near(level, what):
        halo(SIDES, u_copy(level, 0, (0, 1), (0, 1)), what)

    def far_x(level, what):
        halo(SIDES[:2], u_copy(level, 4, (1, 2), (1, 2)), what)

    def far_y(level, what):
        halo(SIDES[2:], u_copy(level, 6, (1, 2), (1, 2)), what)

    def far(level, what):
        if what != "start":
            far_x(level, what)
            far_y(level, what)
            far_c(level, what)

    def far_c(level, what):
        halo(CORNERS, u_copy(level, 8, (0, 2), (0, 3)), what)
        halo(CORNERS, u_copy(level, 12, (2, 1), (0, 1)), what)

    def c_copy(k, h, source):
        to, device = r_peer(k)
        return pltpu.make_async_remote_copy(
            src_ref=cinv_hbm.at[:, pl.ds(pl.multiple_of(h * 2048 + to * 128, 128), 128)],
            dst_ref=cblk.at[pl.ds(source * BLK, BLK), pl.ds(h * 128, 128)],
            send_sem=c_s.at[h, k], recv_sem=c_r.at[h, k],
            device_id=device, device_id_type=MESH)

    def ag_copy(it, k, source):
        return pltpu.make_async_remote_copy(
            src_ref=crow.at[it],
            dst_ref=gath.at[it, pl.ds(source * BLK, BLK)],
            send_sem=ag_s.at[it, k], recv_sem=ag_r.at[it, k],
            device_id=k_peer(k)[1], device_id_type=MESH)

    def rs_copy(it, k, source):
        to, device = r_peer(k)
        return pltpu.make_async_remote_copy(
            src_ref=part.at[it, pl.ds(to * BLK, BLK)],
            dst_ref=recv.at[it, source],
            send_sem=rs_s.at[it, k], recv_sem=rs_r.at[it, k],
            device_id=device, device_id_type=MESH)

    for dx, dy in AROUND:

        @pl.when(~there(dx, dy))
        def _():
            xs = {-1: (0, 3), 0: (3, 16), 1: (19, 3)}[dx]
            ys = {-1: (0, 8), 0: (8, 16), 1: (24, 8)}[dy]
            sig[pl.ds(*xs), pl.ds(*ys)] = jnp.zeros((xs[1], ys[1], 16), F32)

    def spread(columns, copies, inner):
        def one(n, carry):
            x = copies[0] + n + (n // copies[1]) * copies[2]
            if inner:
                sig_t[:, 8 : 8 + B] = jnp.transpose(sig[x, 8 : 8 + B])
            else:
                sig_t[...] = jnp.transpose(sig[x])
            for p in range(2):
                rows = sig_t[pl.ds(p, 8, stride=2), :]
                for y in columns:
                    sig_b[x, y, p] = jnp.broadcast_to(rows[:, y + 5 : y + 6], (8, F))
            return carry

        return one

    own_s.wait()
    lax.fori_loop(0, B, spread(range(3, 3 + B), (3, B, 0), True), 0)

    level = lax.broadcasted_iota(jnp.int32, (8, F), 0)

    def faces(x0, y0, cells):
        s = reader(sig_b, x0, y0, 1)
        done = {}
        for x, y, p in cells:
            if p:
                continue
            even, odd = s(x, y, 0), s(x, y, 1)
            kz_in = 0.5 * (even + odd)
            next_even = jnp.where(level < 7, pltpu.roll(even, 7, 0), 0.0)
            bottom = 0.5 * (odd + next_even)
            kz_out = jnp.where(level < 7, bottom, 0.0)
            above = pltpu.roll(kz_out, 1, 0)
            for q in range(2):
                west = 0.5 * (s(x, y, q) + s(x - 1, y, q))
                east = 0.5 * (s(x, y, q) + s(x + 1, y, q))
                south = 0.5 * (s(x, y, q) + s(x, y - 1, q))
                north = 0.5 * (s(x, y, q) + s(x, y + 1, q))
                depth = (kz_in + above) if q == 0 else (kz_in + bottom)
                d = west + east + south + north + depth
                step = jnp.where(s(x, y, q) > 0.0, OMEGA / jnp.maximum(d, 1e-30), 0.0)
                done[x, y, q] = west, south, (kz_in, kz_out)[q], d, step
        for (x, y, p), values in done.items():
            for ref, value in zip((kx, ky, kz, dg, st), values):
                ref[x0 + x, y0 + y, p] = value

    region(faces, 3, 14, 3, 14, 7, 2)

    own_v.wait()

    def permute(n, carry):
        for y in range(B):
            for p in range(2):
                uu[0, 3 + n, 3 + y, p] = v_nat[n, y, pl.ds(p, 8, stride=2), :]
        return carry

    lax.fori_loop(0, B, permute, 0)

    pl.semaphore_wait(bar, count)
    halo(AROUND, sig_copy, "start")
    near(0, "start")
    far_x(0, "start")
    far_c(0, "start")

    def c_start(k, carry):
        for h in range(2):
            c_copy(k, h, r_at).start()
        return carry

    lax.fori_loop(1, NR, c_start, 0)

    for dx, dy in AROUND:

        @pl.when(~there(dx, dy))
        def _():
            xr = {-1: (0, 3), 0: (3, B), 1: (B + 3, 3)}[dx]
            yr = {-1: (0, 3), 0: (3, B), 1: (B + 3, 3)}[dy]

            def zero_u(n, carry):
                for w in range(ITERS):
                    uu[w, xr[0] + n // yr[1], yr[0] + n % yr[1]] = jnp.zeros((2, 8, F), F32)
                return carry

            lax.fori_loop(0, xr[1] * yr[1], zero_u, 0)

    def zero_ring(n, carry):
        zero = jnp.zeros((2, 8, F), F32)
        bb[0, n] = zero
        bb[E2 + 1, n] = zero
        bb[n, 0] = zero
        bb[n, E2 + 1] = zero
        return carry

    lax.fori_loop(0, E2 + 2, zero_ring, 0)

    corner = (i * B - 2) * (NJ * B) + (j * B - 2)
    source = elec_ref[0:1, :]
    sink = elec_ref[1:2, :]

    def residual(n):
        def body(x0, y0, cells):
            e = reader(uu.at[n], x0, y0, 1)
            fx, fy, fz = (reader(k, x0, y0, 0) for k in (kx, ky, kz))
            done = {}
            for x, y, p in cells:
                value = stencil(e, fx, fy, fz, x, y, p) - dg[x0 + x, y0 + y, p] * e(x, y, p)
                if n > 0:
                    value = rr[x0 + x, y0 + y, p] + value
                elif p == 0:
                    here = corner + (x0 + x) * (NJ * B) + (y0 + y)
                    force = jnp.where(source == here, CURRENT, 0.0) - jnp.where(sink == here, CURRENT, 0.0)
                    value = value + jnp.where(level == 0, jnp.broadcast_to(force, (8, F)), 0.0)
                done[x, y, p] = value, (st[x0 + x, y0 + y, p] * value if n < ITERS else None)
            for (x, y, p), (value, first) in done.items():
                if n < ITERS:
                    rr[x0 + x, y0 + y, p] = value
                    bb[x0 + x + 1, y0 + y + 1, p] = first
                else:
                    res_nat[x0 + x - 2, y0 + y - 2, pl.ds(p, 8, stride=2), :] = value

        return body

    def residual_own_rim(n):
        region(residual(n), 2, 1, 2, 16, 1, 16, 2, 15, 0)
        region(residual(n), 3, 14, 2, 1, 14, 1, 2, 0, 15)

    halo(AROUND, sig_copy, "here")
    lax.fori_loop(0, 6, spread(range(E2 + 2), (0, 3, 16), False), 0)
    lax.fori_loop(0, B, spread((0, 1, 2, 19, 20, 21), (3, B, 0), False), 0)
    region(faces, 0, 3, 0, 20, 3, 10, 2, 17, 0)
    region(faces, 3, 14, 0, 3, 7, 3, 2, 0, 17)

    def last_faces(n, carry):
        for p in range(2):
            kx[E2, n, p] = 0.5 * (sig_b[E2 + 1, n + 1, p] + sig_b[E2, n + 1, p])
            ky[n, E2, p] = 0.5 * (sig_b[n + 1, E2 + 1, p] + sig_b[n + 1, E2, p])
        return carry

    lax.fori_loop(0, E2, last_faces, 0)

    for dx, dy in SIDES:

        @pl.when(~there(dx, dy))
        def _():
            def zero_last(n, carry):
                x = {-1: 2, 0: 3 + n, 1: B + 3}[dx]
                y = {-1: 2, 0: 3 + n, 1: B + 3}[dy]
                uu[ITERS, x, y] = jnp.zeros((2, 8, F), F32)
                return carry

            lax.fori_loop(0, B, zero_last, 0)

    def sweep(src, shift, store):
        def body(x0, y0, cells):
            e = reader(src, x0, y0, shift)
            fx, fy, fz = (reader(k, x0, y0, 0) for k in (kx, ky, kz))
            done = {}
            for x, y, p in cells:
                nearby = stencil(e, fx, fy, fz, x, y, p)
                done[x, y, p] = ((1.0 - OMEGA) * e(x, y, p) + bb[x0 + x + 1, y0 + y + 1, p]
                                 + st[x0 + x, y0 + y, p] * nearby)
            for (x, y, p), value in done.items():
                store(x0 + x, y0 + y, p, value)

        return body

    def into_a(x, y, p, value):
        e_a[x, y, p] = value

    def into_b(x, y, p, value):
        e_b[x, y, p] = value

    def coarse_at(x, y):
        block = ((x - 2) // 4) * 4 + (y - 2) // 4
        return pro[pl.ds(pl.multiple_of(block * 8, 8), 8), :]

    for it in range(ITERS):
        region(residual(it), 3, 14, 3, 14, 7, 2)
        near(it, "here")
        residual_own_rim(it)

        def restrict(n, carry):
            a, b = n // 4, n % 4
            tiles = [rr[2 + 4 * a + x, 2 + 4 * b + y, p] for x in range(4) for y in range(4) for p in range(2)]
            while len(tiles) > 1:
                tiles = [one + two for one, two in zip(tiles[::2], tiles[1::2])]
            acc[pl.ds(pl.multiple_of(n * 8, 8), 8), :] = tiles[0]
            return carry

        lax.fori_loop(0, 16, restrict, 0)
        rows = acc[pl.ds(0, BLK, stride=4), :]
        for q in range(1, 4):
            rows = rows + acc[pl.ds(q, BLK, stride=4), :]
        crow[it] = rows
        gath[it, pl.ds(pl.multiple_of(k_at * BLK, BLK), BLK)] = rows

        def ag_start(k, carry):
            ag_copy(it, k, k_at).start()
            return carry

        lax.fori_loop(1, NK, ag_start, 0)
        far_y(it, "start")

        region(sweep(bb, 1, into_a), 3, 14, 3, 14, 7, 2)
        region(sweep(e_a, 0, into_b), 4, 12, 4, 12, 6, 3)

        def ag_wait(k, carry):
            ag_copy(it, k, lax.rem(k_at - k + NK, NK)).wait_recv()
            return carry

        def into_u(x, y, p, value):
            uu[it + 1, x + 1, y + 1, p] = value

        region(sweep(e_b, 0, into_u), 5, 10, 5, 10, 5, 5)

        if it == 0:
            for copy in own_c:
                copy.wait()

            def c_wait(k, carry):
                for h in range(2):
                    c_copy(k, h, lax.rem(r_at - k + NR, NR)).wait_recv()
                return carry

            lax.fori_loop(1, NR, c_wait, 0)

        lax.fori_loop(1, NK, ag_wait, 0)
        part[it] = jnp.dot(
            cblk[...], gath[it], precision=lax.Precision.HIGHEST, preferred_element_type=F32
        )

        def rs_start(k, carry):
            rs_copy(it, k, r_at).start()
            return carry

        lax.fori_loop(1, NR, rs_start, 0)

        far(it, "here")
        region(residual(it), 0, 2, 0, 20, 2, 10, 2, 18, 0)
        region(residual(it), 2, 16, 0, 2, 8, 2, 2, 0, 18)
        region(sweep(bb, 1, into_a), 0, 3, 0, 20, 3, 10, 2, 17, 0)
        region(sweep(bb, 1, into_a), 3, 14, 0, 3, 7, 3, 2, 0, 17)
        region(sweep(e_a, 0, into_b), 1, 3, 1, 18, 3, 9, 2, 15, 0)
        region(sweep(e_a, 0, into_b), 4, 12, 1, 3, 6, 3, 2, 0, 15)

        def rs_wait(k, carry):
            rs_copy(it, k, lax.rem(r_at - k + NR, NR)).wait_recv()
            return carry

        lax.fori_loop(1, NR, rs_wait, 0)
        recv[it, r_at] = part[it, pl.ds(pl.multiple_of(r_at * BLK, BLK), BLK)]
        total = recv[it, 0]
        for q in range(1, NR):
            total = total + recv[it, q]
        for q in range(4):
            pro[pl.ds(q, BLK, stride=4), :] = total

        def into_u_coarse(x, y, p, value):
            uu[it + 1, x + 1, y + 1, p] = value + coarse_at(x, y)

        region(sweep(e_b, 0, into_u_coarse), 2, 3, 2, 16, 3, 8, 2, 13, 0)
        region(sweep(e_b, 0, into_u_coarse), 5, 10, 2, 3, 10, 3, 2, 0, 13)
        near(it + 1, "start")
        if it + 1 < ITERS:
            far_x(it + 1, "start")
            far_c(it + 1, "start")

        def add_coarse(x0, y0, cells):
            done = {}
            for x, y, p in cells:
                done[x, y, p] = uu[it + 1, x0 + x + 1, y0 + y + 1, p] + coarse_at(x0 + x, y0 + y)
            for (x, y, p), value in done.items():
                uu[it + 1, x0 + x + 1, y0 + y + 1, p] = value

        region(add_coarse, 5, 10, 5, 10, 5, 2)

    def potentials(x0, y0, cells):
        done = {}
        for x, y, p in cells:
            total = uu[0, x0 + x + 1, y0 + y + 1, p]
            for n in range(ITERS):
                total = total + uu[n + 1, x0 + x + 1, y0 + y + 1, p]
            done[x, y, p] = total
        for (x, y, p), value in done.items():
            v_nat[x0 + x - 2, y0 + y - 2, pl.ds(p, 8, stride=2), :] = value

    region(potentials, 2, B, 2, B, 4, 4)
    region(residual(ITERS), 3, 14, 3, 14, 7, 2)
    near(ITERS, "here")
    residual_own_rim(ITERS)

    halo(AROUND, sig_copy, "sent")

    def c_sent(k, carry):
        for h in range(2):
            c_copy(k, h, r_at).wait_send()
        return carry

    lax.fori_loop(1, NR, c_sent, 0)
    near(ITERS, "sent")
    for it in range(ITERS):
        near(it, "sent")
        far(it, "sent")

        def ag_sent(k, carry):
            ag_copy(it, k, k_at).wait_send()
            return carry

        lax.fori_loop(1, NK, ag_sent, 0)

        def rs_sent(k, carry):
            rs_copy(it, k, r_at).wait_send()
            return carry

        lax.fori_loop(1, NR, rs_sent, 0)


def on_device(start_potentials, conductivity, electrodes, coarse_inverse):
    shape = pltpu.VMEM((B, B, B, F), F32)
    tiles = lambda *lead: pltpu.VMEM(tuple(lead) + (2, 8, F), F32)
    dma = pltpu.SemaphoreType.DMA
    anywhere = pl.BlockSpec(memory_space=pl.ANY)
    return pl.pallas_call(
        kernel,
        out_shape=(shape, shape),
        in_specs=[anywhere, anywhere, pl.BlockSpec(memory_space=pltpu.VMEM), anywhere],
        out_specs=(pl.BlockSpec(memory_space=pltpu.VMEM),) * 2,
        scratch_shapes=[
            pltpu.VMEM((22, 32, 16), F32),
            pltpu.VMEM((16, 32), F32),
            tiles(ITERS + 1, 22, 22),
            tiles(20, 20),
            tiles(22, 22),
            tiles(20, 20),
            tiles(20, 20),
            tiles(21, 20),
            tiles(20, 21),
            tiles(20, 20),
            tiles(20, 20),
            tiles(20, 20),
            pltpu.VMEM((512, 256), F32),
            pltpu.VMEM((ITERS, BLK, F), F32),
            pltpu.VMEM((ITERS, 256, F), F32),
            pltpu.VMEM((ITERS, 512, F), F32),
            pltpu.VMEM((ITERS, NR, BLK, F), F32),
            pltpu.VMEM((128, F), F32),
            pltpu.VMEM((128, F), F32),
            dma((8,)), dma((8,)),
            dma((ITERS + 1, 16)), dma((ITERS + 1, 16)),
            dma((2, NR)), dma((2, NR)),
            dma((ITERS, NK)), dma((ITERS, NK)),
            dma((ITERS, NR)), dma((ITERS, NR)),
            dma((4,)),
        ],
        compiler_params=pltpu.CompilerParams(
            collective_id=0, has_side_effects=True, vmem_limit_bytes=50 * 2**20
        ),
        cost_estimate=pl.CostEstimate(flops=10**8, bytes_accessed=10**7, transcendentals=0),
    )(start_potentials, conductivity, electrodes.T, coarse_inverse)


def solution(mesh):
    in_specs = (P("gx", "gy", None, None), P("gx", "gy", None), P(), P(("gx", "gy"), None))
    out_specs = (P("gx", "gy", None, None), P("gx", "gy", None, None))
    return jax.shard_map(
        on_device, mesh=mesh, in_specs=in_specs, out_specs=out_specs, check_vma=False
    )
```

```python
import jax
import jax.numpy as jnp
from jax import lax
from jax.experimental import pallas as pl
from jax.experimental.pallas import tpu as pltpu
from jax.sharding import PartitionSpec as P

OMEGA = 0.7
CURRENT = 8.0
ITERS = 2
NI, NJ = 8, 16
NK, NR = 8, 16
B = 16
F = 128
E2 = B + 4
BLK = 32
MESH = pl.DeviceIdType.MESH
F32 = jnp.float32

SIDES = ((-1, 0), (1, 0), (0, -1), (0, 1))
CORNERS = ((-1, -1), (-1, 1), (1, -1), (1, 1))
AROUND = SIDES + CORNERS


def stencil(e, kx, ky, kz, x, y, p):
    total = kx(x, y, p) * e(x - 1, y, p) + kx(x + 1, y, p) * e(x + 1, y, p)
    total = total + (ky(x, y, p) * e(x, y - 1, p) + ky(x, y + 1, p) * e(x, y + 1, p))
    other = e(x, y, 1 - p)
    if p == 0:
        across = pltpu.roll(kz(x, y, 1) * other, 1, 0)
    else:
        across = kz(x, y, 1) * pltpu.roll(other, 7, 0)
    return total + (kz(x, y, 0) * other + across)


def reader(ref, x0, y0, shift):
    held = {}

    def get(x, y, p):
        key = (x, y, p)
        if key not in held:
            held[key] = ref[x0 + (x + shift), y0 + (y + shift), p]
        return held[key]

    return get


def region(body, x_lo, x_n, y_lo, y_n, xb, yb, copies=1, step_x=0, step_y=0):
    nx, ny = x_n // xb, y_n // yb
    assert nx * xb == x_n and ny * yb == y_n
    cells = [(x, y, p) for x in range(xb) for y in range(yb) for p in range(2)]

    def one(n, carry):
        x0, y0 = x_lo, y_lo
        if copies > 1:
            side = n // (nx * ny)
            x0, y0 = x0 + side * step_x, y0 + side * step_y
            n = n % (nx * ny) if nx * ny > 1 else 0
        if nx > 1:
            x0 = x0 + (n // ny) * xb
        if ny > 1:
            y0 = y0 + ((n % ny) if nx > 1 else n) * yb
        body(x0, y0, cells)
        return carry

    lax.fori_loop(0, copies * nx * ny, one, 0)


def kernel(
    v_hbm, cond_ref, elec_ref, cinv_hbm,
    v_nat, res_nat,
    sig, sig_t, uu, rr, bb, e_a, e_b, kx, ky, kz, st, dg,
    cblk, crow, gath, part, recv, pro, acc,
    sig_s, sig_r, u_s, u_r, c_s, c_r, ag_s, ag_r, rs_s, rs_r, loc,
):
    i = lax.axis_index("gx")
    j = lax.axis_index("gy")
    high, y_at = i // 4, lax.rem(i, 4)
    z_at, low = j // 4, lax.rem(j, 4)
    k_at = high * 4 + low
    r_at = y_at * 4 + z_at
    sig_b = uu.at[ITERS]

    def there(dx, dy):
        ok = None
        for d, pos, n in ((dx, i, NI), (dy, j, NJ)):
            if d:
                term = (pos > 0) if d < 0 else (pos < n - 1)
                ok = term if ok is None else ok & term
        return ok

    bar = pltpu.get_barrier_semaphore()

    def greet(to_i, to_j):
        pl.semaphore_signal(bar, inc=1, device_id=(to_i, to_j), device_id_type=MESH)

    def k_peer(k):
        to = lax.rem(k_at + k, NK)
        return to, ((to // 4) * 4 + y_at, z_at * 4 + lax.rem(to, 4))

    def r_peer(k):
        to = lax.rem(r_at + k, NR)
        return to, (high * 4 + to // 4, lax.rem(to, 4) * 4 + low)

    count = jnp.int32(NK - 1 + NR - 1)
    for dx, dy in AROUND:
        ok = there(dx, dy)
        if dy == 0:
            ok = ok & ((i + dx) // 4 != high)
        if dx == 0:
            ok = ok & ((j + dy) // 4 != z_at)

        @pl.when(ok)
        def _():
            greet(i + dx, j + dy)

        count = count + jnp.where(ok, 1, 0)

    def greet_k(k, carry):
        greet(*k_peer(k)[1])
        return carry

    def greet_r(k, carry):
        greet(*r_peer(k)[1])
        return carry

    lax.fori_loop(1, NK, greet_k, 0)
    lax.fori_loop(1, NR, greet_r, 0)

    own_s = pltpu.make_async_copy(cond_ref, sig.at[pl.ds(3, B), pl.ds(8, B)], loc.at[2])
    own_s.start()
    own_v = pltpu.make_async_copy(v_hbm, v_nat, loc.at[3])
    own_v.start()
    own_c = [
        pltpu.make_async_copy(
            cinv_hbm.at[:, pl.ds(pl.multiple_of(h * 2048 + r_at * 128, 128), 128)],
            cblk.at[pl.ds(r_at * BLK, BLK), pl.ds(h * 128, 128)],
            loc.at[h],
        )
        for h in range(2)
    ]
    for copy in own_c:
        copy.start()

    def halo(dirs, make, what):
        for n, (dx, dy) in enumerate(dirs):
            if what in ("start", "sent"):

                @pl.when(there(dx, dy))
                def _():
                    copy = make(n, dx, dy)
                    copy.start() if what == "start" else copy.wait_send()

            else:

                @pl.when(there(-dx, -dy))
                def _():
                    make(n, dx, dy).wait_recv()

    def sig_copy(n, dx, dy):
        xs = {-1: (3, 3, 19), 0: (3, 16, 3), 1: (16, 3, 0)}[dx]
        ys = {-1: (8, 8, 24), 0: (8, 16, 8), 1: (16, 8, 0)}[dy]
        src = cond_ref.at[pl.ds(xs[0] - 3, xs[1]), pl.ds(ys[0] - 8, ys[1])]
        dst = sig.at[pl.ds(xs[2], xs[1]), pl.ds(ys[2], ys[1])]
        return pltpu.make_async_remote_copy(
            src_ref=src, dst_ref=dst, send_sem=sig_s.at[n], recv_sem=sig_r.at[n],
            device_id=(i + dx, j + dy), device_id_type=MESH)

    def u_copy(level, base, x_layers, y_layers):
        def span(d, layers):
            if d == 0:
                return 3, B, 3
            first, number = layers
            start = 3 + first if d < 0 else 3 + B - first - number
            return start, number, start - d * B

        def make(n, dx, dy):
            xs, ys = span(dx, x_layers), span(dy, y_layers)
            return pltpu.make_async_remote_copy(
                src_ref=uu.at[level, pl.ds(xs[0], xs[1]), pl.ds(ys[0], ys[1])],
                dst_ref=uu.at[level, pl.ds(xs[2], xs[1]), pl.ds(ys[2], ys[1])],
                send_sem=u_s.at[level, base + n], recv_sem=u_r.at[level, base + n],
                device_id=(i + dx, j + dy), device_id_type=MESH)

        return make

    def near(level, what):
        halo(SIDES, u_copy(level, 0, (0, 1), (0, 1)), what)

    def far_x(level, what):
        halo(SIDES[:2], u_copy(level, 4, (1, 2), (1, 2)), what)

    def far_y(level, what):
        halo(SIDES[2:], u_copy(level, 6, (1, 2), (1, 2)), what)

    def far(level, what):
        if what != "start":
            far_x(level, what)
            far_y(level, what)
            far_c(level, what)

    def far_c(level, what):
        halo(CORNERS, u_copy(level, 8, (0, 2), (0, 3)), what)
        halo(CORNERS, u_copy(level, 12, (2, 1), (0, 1)), what)

    def c_copy(k, h, source):
        to, device = r_peer(k)
        return pltpu.make_async_remote_copy(
            src_ref=cinv_hbm.at[:, pl.ds(pl.multiple_of(h * 2048 + to * 128, 128), 128)],
            dst_ref=cblk.at[pl.ds(source * BLK, BLK), pl.ds(h * 128, 128)],
            send_sem=c_s.at[h, k], recv_sem=c_r.at[h, k],
            device_id=device, device_id_type=MESH)

    def ag_copy(it, k, source):
        return pltpu.make_async_remote_copy(
            src_ref=crow.at[it],
            dst_ref=gath.at[it, pl.ds(source * BLK, BLK)],
            send_sem=ag_s.at[it, k], recv_sem=ag_r.at[it, k],
            device_id=k_peer(k)[1], device_id_type=MESH)

    def rs_copy(it, k, source):
        to, device = r_peer(k)
        return pltpu.make_async_remote_copy(
            src_ref=part.at[it, pl.ds(to * BLK, BLK)],
            dst_ref=recv.at[it, source],
            send_sem=rs_s.at[it, k], recv_sem=rs_r.at[it, k],
            device_id=device, device_id_type=MESH)

    for dx, dy in AROUND:

        @pl.when(~there(dx, dy))
        def _():
            xs = {-1: (0, 3), 0: (3, 16), 1: (19, 3)}[dx]
            ys = {-1: (0, 8), 0: (8, 16), 1: (24, 8)}[dy]
            sig[pl.ds(*xs), pl.ds(*ys)] = jnp.zeros((xs[1], ys[1], 16), F32)

    def spread(columns, copies, inner):
        def one(n, carry):
            x = copies[0] + n + (n // copies[1]) * copies[2]
            if inner:
                sig_t[:, 8 : 8 + B] = jnp.transpose(sig[x, 8 : 8 + B])
            else:
                sig_t[...] = jnp.transpose(sig[x])
            for p in range(2):
                rows = sig_t[pl.ds(p, 8, stride=2), :]
                for y in columns:
                    sig_b[x, y, p] = jnp.broadcast_to(rows[:, y + 5 : y + 6], (8, F))
            return carry

        return one

    own_s.wait()
    lax.fori_loop(0, B, spread(range(3, 3 + B), (3, B, 0), True), 0)

    level = lax.broadcasted_iota(jnp.int32, (8, F), 0)

    def faces(x0, y0, cells):
        s = reader(sig_b, x0, y0, 1)
        done = {}
        for x, y, p in cells:
            if p:
                continue
            even, odd = s(x, y, 0), s(x, y, 1)
            kz_in = 0.5 * (even + odd)
            next_even = jnp.where(level < 7, pltpu.roll(even, 7, 0), 0.0)
            bottom = 0.5 * (odd + next_even)
            kz_out = jnp.where(level < 7, bottom, 0.0)
            above = pltpu.roll(kz_out, 1, 0)
            for q in range(2):
                west = 0.5 * (s(x, y, q) + s(x - 1, y, q))
                east = 0.5 * (s(x, y, q) + s(x + 1, y, q))
                south = 0.5 * (s(x, y, q) + s(x, y - 1, q))
                north = 0.5 * (s(x, y, q) + s(x, y + 1, q))
                depth = (kz_in + above) if q == 0 else (kz_in + bottom)
                d = west + east + south + north + depth
                step = jnp.where(s(x, y, q) > 0.0, OMEGA / jnp.maximum(d, 1e-30), 0.0)
                done[x, y, q] = west, south, (kz_in, kz_out)[q], d, step
        for (x, y, p), values in done.items():
            for ref, value in zip((kx, ky, kz, dg, st), values):
                ref[x0 + x, y0 + y, p] = value

    region(faces, 3, 14, 3, 14, 7, 2)

    own_v.wait()

    def permute(n, carry):
        for y in range(B):
            for p in range(2):
                uu[0, 3 + n, 3 + y, p] = v_nat[n, y, pl.ds(p, 8, stride=2), :]
        return carry

    lax.fori_loop(0, B, permute, 0)

    pl.semaphore_wait(bar, count)
    halo(AROUND, sig_copy, "start")
    near(0, "start")
    far_x(0, "start")
    far_c(0, "start")

    def c_start(k, carry):
        for h in range(2):
            c_copy(k, h, r_at).start()
        return carry

    lax.fori_loop(1, NR, c_start, 0)

    for dx, dy in AROUND:

        @pl.when(~there(dx, dy))
        def _():
            xr = {-1: (0, 3), 0: (3, B), 1: (B + 3, 3)}[dx]
            yr = {-1: (0, 3), 0: (3, B), 1: (B + 3, 3)}[dy]

            def zero_u(n, carry):
                for w in range(ITERS):
                    uu[w, xr[0] + n // yr[1], yr[0] + n % yr[1]] = jnp.zeros((2, 8, F), F32)
                return carry

            lax.fori_loop(0, xr[1] * yr[1], zero_u, 0)

    def zero_ring(n, carry):
        zero = jnp.zeros((2, 8, F), F32)
        bb[0, n] = zero
        bb[E2 + 1, n] = zero
        bb[n, 0] = zero
        bb[n, E2 + 1] = zero
        return carry

    lax.fori_loop(0, E2 + 2, zero_ring, 0)

    corner = (i * B - 2) * (NJ * B) + (j * B - 2)
    source = elec_ref[0:1, :]
    sink = elec_ref[1:2, :]

    def residual(n):
        def body(x0, y0, cells):
            e = reader(uu.at[n], x0, y0, 1)
            fx, fy, fz = (reader(k, x0, y0, 0) for k in (kx, ky, kz))
            done = {}
            for x, y, p in cells:
                value = stencil(e, fx, fy, fz, x, y, p) - dg[x0 + x, y0 + y, p] * e(x, y, p)
                if n > 0:
                    value = rr[x0 + x, y0 + y, p] + value
                elif p == 0:
                    here = corner + (x0 + x) * (NJ * B) + (y0 + y)
                    force = jnp.where(source == here, CURRENT, 0.0) - jnp.where(sink == here, CURRENT, 0.0)
                    value = value + jnp.where(level == 0, jnp.broadcast_to(force, (8, F)), 0.0)
                done[x, y, p] = value, (st[x0 + x, y0 + y, p] * value if n < ITERS else None)
            for (x, y, p), (value, first) in done.items():
                if n < ITERS:
                    rr[x0 + x, y0 + y, p] = value
                    bb[x0 + x + 1, y0 + y + 1, p] = first
                else:
                    res_nat[x0 + x - 2, y0 + y - 2, pl.ds(p, 8, stride=2), :] = value

        return body

    def residual_own_rim(n):
        region(residual(n), 2, 1, 2, 16, 1, 16, 2, 15, 0)
        region(residual(n), 3, 14, 2, 1, 14, 1, 2, 0, 15)

    halo(AROUND, sig_copy, "here")
    lax.fori_loop(0, 6, spread(range(E2 + 2), (0, 3, 16), False), 0)
    lax.fori_loop(0, B, spread((0, 1, 2, 19, 20, 21), (3, B, 0), False), 0)
    region(faces, 0, 3, 0, 20, 3, 10, 2, 17, 0)
    region(faces, 3, 14, 0, 3, 7, 3, 2, 0, 17)

    def last_faces(n, carry):
        for p in range(2):
            kx[E2, n, p] = 0.5 * (sig_b[E2 + 1, n + 1, p] + sig_b[E2, n + 1, p])
            ky[n, E2, p] = 0.5 * (sig_b[n + 1, E2 + 1, p] + sig_b[n + 1, E2, p])
        return carry

    lax.fori_loop(0, E2, last_faces, 0)

    for dx, dy in SIDES:

        @pl.when(~there(dx, dy))
        def _():
            def zero_last(n, carry):
                x = {-1: 2, 0: 3 + n, 1: B + 3}[dx]
                y = {-1: 2, 0: 3 + n, 1: B + 3}[dy]
                uu[ITERS, x, y] = jnp.zeros((2, 8, F), F32)
                return carry

            lax.fori_loop(0, B, zero_last, 0)

    def sweep(src, shift, store):
        def body(x0, y0, cells):
            e = reader(src, x0, y0, shift)
            fx, fy, fz = (reader(k, x0, y0, 0) for k in (kx, ky, kz))
            done = {}
            for x, y, p in cells:
                nearby = stencil(e, fx, fy, fz, x, y, p)
                done[x, y, p] = ((1.0 - OMEGA) * e(x, y, p) + bb[x0 + x + 1, y0 + y + 1, p]
                                 + st[x0 + x, y0 + y, p] * nearby)
            for (x, y, p), value in done.items():
                store(x0 + x, y0 + y, p, value)

        return body

    def into_a(x, y, p, value):
        e_a[x, y, p] = value

    def into_b(x, y, p, value):
        e_b[x, y, p] = value

    def coarse_at(x, y):
        block = ((x - 2) // 4) * 4 + (y - 2) // 4
        return pro[pl.ds(pl.multiple_of(block * 8, 8), 8), :]

    for it in range(ITERS):
        region(residual(it), 3, 14, 3, 14, 7, 2)
        near(it, "here")
        far_y(it, "start")
        residual_own_rim(it)

        def restrict(n, carry):
            a, b = n // 4, n % 4
            tiles = [rr[2 + 4 * a + x, 2 + 4 * b + y, p] for x in range(4) for y in range(4) for p in range(2)]
            while len(tiles) > 1:
                tiles = [one + two for one, two in zip(tiles[::2], tiles[1::2])]
            acc[pl.ds(pl.multiple_of(n * 8, 8), 8), :] = tiles[0]
            return carry

        lax.fori_loop(0, 16, restrict, 0)
        rows = acc[pl.ds(0, BLK, stride=4), :]
        for q in range(1, 4):
            rows = rows + acc[pl.ds(q, BLK, stride=4), :]
        crow[it] = rows
        gath[it, pl.ds(pl.multiple_of(k_at * BLK, BLK), BLK)] = rows

        def ag_start(k, carry):
            ag_copy(it, k, k_at).start()
            return carry

        lax.fori_loop(1, NK, ag_start, 0)

        region(sweep(bb, 1, into_a), 3, 14, 3, 14, 7, 2)
        region(sweep(e_a, 0, into_b), 4, 12, 4, 12, 6, 3)

        def ag_wait(k, carry):
            ag_copy(it, k, lax.rem(k_at - k + NK, NK)).wait_recv()
            return carry

        def into_u(x, y, p, value):
            uu[it + 1, x + 1, y + 1, p] = value

        region(sweep(e_b, 0, into_u), 5, 10, 5, 10, 5, 5)

        if it == 0:
            for copy in own_c:
                copy.wait()

            def c_wait(k, carry):
                for h in range(2):
                    c_copy(k, h, lax.rem(r_at - k + NR, NR)).wait_recv()
                return carry

            lax.fori_loop(1, NR, c_wait, 0)

        lax.fori_loop(1, NK, ag_wait, 0)
        part[it] = jnp.dot(
            cblk[...], gath[it], precision=lax.Precision.HIGHEST, preferred_element_type=F32
        )

        def rs_start(k, carry):
            rs_copy(it, k, r_at).start()
            return carry

        lax.fori_loop(1, NR, rs_start, 0)

        far(it, "here")
        region(residual(it), 0, 2, 0, 20, 2, 10, 2, 18, 0)
        region(residual(it), 2, 16, 0, 2, 8, 2, 2, 0, 18)
        region(sweep(bb, 1, into_a), 0, 3, 0, 20, 3, 10, 2, 17, 0)
        region(sweep(bb, 1, into_a), 3, 14, 0, 3, 7, 3, 2, 0, 17)
        region(sweep(e_a, 0, into_b), 1, 3, 1, 18, 3, 9, 2, 15, 0)
        region(sweep(e_a, 0, into_b), 4, 12, 1, 3, 6, 3, 2, 0, 15)

        def rs_wait(k, carry):
            rs_copy(it, k, lax.rem(r_at - k + NR, NR)).wait_recv()
            return carry

        lax.fori_loop(1, NR, rs_wait, 0)
        recv[it, r_at] = part[it, pl.ds(pl.multiple_of(r_at * BLK, BLK), BLK)]
        total = recv[it, 0]
        for q in range(1, NR):
            total = total + recv[it, q]
        for q in range(4):
            pro[pl.ds(q, BLK, stride=4), :] = total

        def into_u_coarse(x, y, p, value):
            uu[it + 1, x + 1, y + 1, p] = value + coarse_at(x, y)

        region(sweep(e_b, 0, into_u_coarse), 2, 3, 2, 16, 3, 8, 2, 13, 0)
        region(sweep(e_b, 0, into_u_coarse), 5, 10, 2, 3, 10, 3, 2, 0, 13)
        near(it + 1, "start")
        if it + 1 < ITERS:
            far_x(it + 1, "start")
            far_c(it + 1, "start")

        def add_coarse(x0, y0, cells):
            done = {}
            for x, y, p in cells:
                done[x, y, p] = uu[it + 1, x0 + x + 1, y0 + y + 1, p] + coarse_at(x0 + x, y0 + y)
            for (x, y, p), value in done.items():
                uu[it + 1, x0 + x + 1, y0 + y + 1, p] = value

        region(add_coarse, 5, 10, 5, 10, 5, 2)

    def potentials(x0, y0, cells):
        done = {}
        for x, y, p in cells:
            total = uu[0, x0 + x + 1, y0 + y + 1, p]
            for n in range(ITERS):
                total = total + uu[n + 1, x0 + x + 1, y0 + y + 1, p]
            done[x, y, p] = total
        for (x, y, p), value in done.items():
            v_nat[x0 + x - 2, y0 + y - 2, pl.ds(p, 8, stride=2), :] = value

    region(potentials, 2, B, 2, B, 4, 4)
    region(residual(ITERS), 3, 14, 3, 14, 7, 2)
    near(ITERS, "here")
    residual_own_rim(ITERS)

    halo(AROUND, sig_copy, "sent")

    def c_sent(k, carry):
        for h in range(2):
            c_copy(k, h, r_at).wait_send()
        return carry

    lax.fori_loop(1, NR, c_sent, 0)
    near(ITERS, "sent")
    for it in range(ITERS):
        near(it, "sent")
        far(it, "sent")

        def ag_sent(k, carry):
            ag_copy(it, k, k_at).wait_send()
            return carry

        lax.fori_loop(1, NK, ag_sent, 0)

        def rs_sent(k, carry):
            rs_copy(it, k, r_at).wait_send()
            return carry

        lax.fori_loop(1, NR, rs_sent, 0)


def on_device(start_potentials, conductivity, electrodes, coarse_inverse):
    shape = pltpu.VMEM((B, B, B, F), F32)
    tiles = lambda *lead: pltpu.VMEM(tuple(lead) + (2, 8, F), F32)
    dma = pltpu.SemaphoreType.DMA
    anywhere = pl.BlockSpec(memory_space=pl.ANY)
    return pl.pallas_call(
        kernel,
        out_shape=(shape, shape),
        in_specs=[anywhere, anywhere, pl.BlockSpec(memory_space=pltpu.VMEM), anywhere],
        out_specs=(pl.BlockSpec(memory_space=pltpu.VMEM),) * 2,
        scratch_shapes=[
            pltpu.VMEM((22, 32, 16), F32),
            pltpu.VMEM((16, 32), F32),
            tiles(ITERS + 1, 22, 22),
            tiles(20, 20),
            tiles(22, 22),
            tiles(20, 20),
            tiles(20, 20),
            tiles(21, 20),
            tiles(20, 21),
            tiles(20, 20),
            tiles(20, 20),
            tiles(20, 20),
            pltpu.VMEM((512, 256), F32),
            pltpu.VMEM((ITERS, BLK, F), F32),
            pltpu.VMEM((ITERS, 256, F), F32),
            pltpu.VMEM((ITERS, 512, F), F32),
            pltpu.VMEM((ITERS, NR, BLK, F), F32),
            pltpu.VMEM((128, F), F32),
            pltpu.VMEM((128, F), F32),
            dma((8,)), dma((8,)),
            dma((ITERS + 1, 16)), dma((ITERS + 1, 16)),
            dma((2, NR)), dma((2, NR)),
            dma((ITERS, NK)), dma((ITERS, NK)),
            dma((ITERS, NR)), dma((ITERS, NR)),
            dma((4,)),
        ],
        compiler_params=pltpu.CompilerParams(
            collective_id=0, has_side_effects=True, vmem_limit_bytes=50 * 2**20
        ),
        cost_estimate=pl.CostEstimate(flops=10**8, bytes_accessed=10**7, transcendentals=0),
    )(start_potentials, conductivity, electrodes.T, coarse_inverse)


def solution(mesh):
    in_specs = (P("gx", "gy", None, None), P("gx", "gy", None), P(), P(("gx", "gy"), None))
    out_specs = (P("gx", "gy", None, None), P("gx", "gy", None, None))
    return jax.shard_map(
        on_device, mesh=mesh, in_specs=in_specs, out_specs=out_specs, check_vma=False
    )
```
